32 devices in a mesh: tm: 8 (over z, y), space: 4 (over x, core).
Axes of the slice: x: 2, y: 2, z: 4, core: 2. Of those that a mesh axis runs over, the one named last changes fastest.
Arguments:
- snapshots: float32 [1024, 32, 2048], P('tm', None, 'space'), may hold values from -12 to 12
- quad_weights: float32 [2048], P('space'), may hold values from 0.25 to 4
Outputs:
- modes: float32 [2, 1024, 2048], P(None, 'tm', 'space')
- energies: float32 [1024], P('tm')
The draws below stay inside these ranges and needn't reach their ends.
All inputs are finite; a program needn't handle non-finite values.
Results may differ from the reference program's by a relative error of at most 0.0001.
Values sent between devices are 32-bit elements; how exact they have to be, the bound alone decides.
No kernel may reach another device: no remote copies, remote signals or barrier semaphores. Data moves between devices by JAX's collectives and lax.ppermute only.
A program may use at most 128 MiB of HBM per device.

```python
import math
import jax
import jax.numpy as jnp
from jax import lax

NT = 1024
B = 32
POWER = 3
NT_DEV = 128
NS = 2048
N_TM = 8


def draw_snapshots(key, part):
    key_noise, key_common, key_amp = jax.random.split(key, 3)
    noise = jnp.clip(jax.random.normal(key_noise, (NT, B, NS), jnp.float32), -6.0, 6.0)
    common = jnp.clip(jax.random.normal(key_common, (NT, 1, NS), jnp.float32), -6.0, 6.0)
    amplitude = jax.random.uniform(key_amp, (1, B, 1), jnp.float32, 0.15, 0.5)
    return (noise + amplitude * common).astype(jnp.float32)


def block_scale(stream_key, extent, cuts, smallest, largest):
    gain = 1.0
    for dim, blocks in cuts:
        steps = jax.random.uniform(jax.random.fold_in(jax.random.fold_in(stream_key, 6), dim), (blocks,), jnp.float32, smallest / len(cuts), largest / len(cuts))
        gain = gain * jnp.repeat(jnp.exp(steps), extent[dim] // blocks).reshape((-1,) + (1,) * (len(extent) - 1 - dim))
    return gain


def setup_inputs(seed: int = 0) -> dict:
    arg_keys = jax.random.split(jax.random.key(seed), 3)
    return {
        "snapshots": draw_snapshots(jax.random.fold_in(arg_keys[2], 71), 0),
        "quad_weights": jnp.clip(jnp.exp(math.log(4.0) - 2.7725887 * jax.random.uniform(arg_keys[1], (NS,), jnp.float32) ** block_scale(arg_keys[1], (NS,), ((0, 4),), -0.2, 0.2)), 0.25, 4.0),
    }


def bit_reverse(values, bit_count):
    result = jnp.zeros_like(values)
    for position in range(bit_count):
        result = result + ((values >> position & 1) << bit_count - 1 - position)
    return result

def matvec(matrix, vector):
    return jnp.einsum('fbc,fc->fb', matrix, vector, precision=lax.Precision.HIGHEST)

def power_modes(real_gram, imag_gram):
    vec_real = jnp.ones(real_gram.shape[:2], jnp.float32) / math.sqrt(real_gram.shape[1])
    vec_imag = jnp.zeros(real_gram.shape[:2], jnp.float32)
    for sweep_idx in range(POWER):
        new_real = matvec(real_gram, vec_real) - matvec(imag_gram, vec_imag)
        new_imag = matvec(real_gram, vec_imag) + matvec(imag_gram, vec_real)
        length = lax.rsqrt(lax.optimization_barrier(jnp.sum(new_real * new_real + new_imag * new_imag, axis=1, keepdims=True)) + 1e-06)
        vec_real = new_real * length
        vec_imag = new_imag * length
    image_real = matvec(real_gram, vec_real) - matvec(imag_gram, vec_imag)
    image_imag = matvec(real_gram, vec_imag) + matvec(imag_gram, vec_real)
    energy = lax.optimization_barrier(jnp.sum(vec_real * image_real + vec_imag * image_imag, axis=1))
    return (vec_real, vec_imag, energy)

def reference(snapshots, quad_weights):
    time_ids = jnp.arange(NT).astype(jnp.float32)
    window = (0.5 - 0.5 * jnp.cos(2.0 * math.pi * time_ids / NT)) / math.sqrt(0.375 * NT)
    spectrum = jnp.fft.fft(snapshots * window[:, None, None], axis=0)
    row_ids = jnp.arange(NT, dtype=jnp.int32)
    bit_count = N_TM.bit_length() - 1
    reorder = bit_reverse(row_ids // NT_DEV, bit_count) + N_TM * (row_ids % NT_DEV)
    spectrum = spectrum[reorder]
    spectral = jnp.stack([jnp.real(spectrum), jnp.imag(spectrum)]).astype(jnp.float32)
    weighted = spectral * quad_weights
    gram_full = jnp.einsum('pfbx,qfcx->fpbqc', weighted, spectral, precision=lax.Precision.HIGHEST) / NS
    real_gram = gram_full[:, 0, :, 0] + gram_full[:, 1, :, 1]
    imag_gram = gram_full[:, 0, :, 1] - gram_full[:, 1, :, 0]
    vec_real, vec_imag, energy = power_modes(real_gram, imag_gram)
    inverse_root = lax.rsqrt(energy + 1e-06)[:, None]
    modes_real = jnp.einsum('fb,fbx->fx', vec_real, spectral[0], precision=lax.Precision.HIGHEST) - jnp.einsum('fb,fbx->fx', vec_imag, spectral[1], precision=lax.Precision.HIGHEST)
    modes_imag = jnp.einsum('fb,fbx->fx', vec_imag, spectral[0], precision=lax.Precision.HIGHEST) + jnp.einsum('fb,fbx->fx', vec_real, spectral[1], precision=lax.Precision.HIGHEST)
    return (jnp.stack([modes_real * inverse_root, modes_imag * inverse_root]), energy)
```

```python
import functools
import math

import jax
import jax.numpy as jnp
import ml_dtypes
import numpy as np
from jax import lax
from jax.experimental import pallas as pl
from jax.experimental.pallas import tpu as pltpu
from jax.sharding import PartitionSpec as P

POWER = 3
CHUNK = 8
HALF = 64
LANES = 128
BF16 = jnp.bfloat16
F32 = jnp.float32


def bit_reverse(value, bit_count):
    return sum((value >> i & 1) << (bit_count - 1 - i) for i in range(bit_count))


def split_np(table):
    high = table.astype(ml_dtypes.bfloat16)
    low = (table - high.astype(np.float64)).astype(ml_dtypes.bfloat16)
    return high, low


def split(value):
    high = value.astype(BF16)
    return high, (value - high.astype(F32)).astype(BF16)


def low_half(shape):
    return lax.broadcasted_iota(jnp.int32, shape, len(shape) - 1) < HALF


def params(mib):
    return pltpu.CompilerParams(vmem_limit_bytes=mib * 2**20)


@functools.lru_cache(None)
def transform_tables(total_times, slots, tile):
    t = np.arange(total_times)
    window = (0.5 - 0.5 * np.cos(2 * np.pi * t / total_times)) / math.sqrt(0.375 * total_times)
    k = np.arange(slots)
    phase = 2 * np.pi * (k[:, None] * t[None, :] % total_times) / total_times
    live = (k <= total_times // 2)[:, None]
    real = np.cos(phase) * window * live
    imag = -np.sin(phase) * window * live
    both = np.stack([real, imag]).reshape(2, slots // tile, tile, total_times)
    both = both.transpose(1, 0, 2, 3).reshape(2 * slots, total_times)
    return split_np(both)


@functools.lru_cache(None)
def output_order(total_times, tm_size, slots):
    local = total_times // tm_size
    bits = tm_size.bit_length() - 1
    q = np.arange(total_times)
    freq = np.array([bit_reverse(d, bits) for d in range(tm_size)])[q // local]
    freq = freq + tm_size * (q % local)
    mirrored = freq > total_times // 2
    slot = np.where(mirrored, total_times - freq, freq)
    onehot = (slot[:, None] == np.arange(slots)[None, :]).astype(ml_dtypes.bfloat16)
    sign = np.where(mirrored, -1.0, 1.0).astype(np.float32)
    lanes = np.ones((total_times, LANES), np.float32)
    lanes[:, HALF:] = sign[:, None]
    return onehot, lanes


def pack_kernel(x_ref, out_ref):
    times = x_ref.shape[0]
    rows = x_ref.reshape(times * CHUNK, LANES)
    low = low_half((times, LANES))
    for j in range(CHUNK // 2):
        first = rows[pl.ds(j, times, stride=CHUNK), :]
        second = rows[pl.ds(j + CHUNK // 2, times, stride=CHUNK), :]
        cols = slice(j * LANES, (j + 1) * LANES)
        out_ref[0, :, cols] = jnp.where(low, first, pltpu.roll(second, HALF, 1))
        out_ref[1, :, cols] = jnp.where(low, pltpu.roll(first, HALF, 1), second)


def pack(snapshots, chunk, tm_size):
    times, _, points = snapshots.shape
    width = CHUNK * HALF
    return pl.pallas_call(
        pack_kernel,
        grid=(points // LANES,),
        in_specs=[pl.BlockSpec((times, CHUNK, LANES), lambda i: (0, chunk, i))],
        out_specs=pl.BlockSpec((2, times, width), lambda i: (i, 0, 0)),
        out_shape=jax.ShapeDtypeStruct((tm_size, times, width), F32),
        compiler_params=params(32),
        name="pack",
    )(snapshots)


def transform_kernel(tile, high_ref, low_ref, x_ref, out_ref, xh_ref, xl_ref):
    @pl.when(pl.program_id(0) == 0)
    def _():
        high, low = split(x_ref[...])
        xh_ref[...] = high
        xl_ref[...] = low

    dot = functools.partial(jnp.dot, preferred_element_type=F32)
    both = dot(high_ref[...], xh_ref[...])
    both = both + dot(high_ref[...], xl_ref[...])
    both = both + dot(low_ref[...], xh_ref[...])
    low = low_half((tile, LANES))
    for j in range(CHUNK // 2):
        cols = slice(j * LANES, (j + 1) * LANES)
        real, imag = both[:tile, cols], both[tile:, cols]
        out_ref[pl.ds(j, tile, stride=CHUNK), :] = jnp.where(low, real, pltpu.roll(imag, HALF, 1))
        out_ref[pl.ds(j + CHUNK // 2, tile, stride=CHUNK), :] = jnp.where(
            low, pltpu.roll(real, HALF, 1), imag
        )


def transform(columns, tables, slots, tile):
    total, width = columns.shape
    return pl.pallas_call(
        functools.partial(transform_kernel, tile),
        grid=(slots // tile,),
        in_specs=[
            pl.BlockSpec((2 * tile, total), lambda i: (i, 0)),
            pl.BlockSpec((2 * tile, total), lambda i: (i, 0)),
            pl.BlockSpec((total, width), lambda i: (0, 0)),
        ],
        out_specs=pl.BlockSpec((tile * CHUNK, LANES), lambda i: (i, 0)),
        out_shape=jax.ShapeDtypeStruct((slots * CHUNK, LANES), F32),
        scratch_shapes=[pltpu.VMEM((total, width), BF16)] * 2,
        compiler_params=params(48),
        name="transform",
    )(*tables, columns)


def gram_kernel(tile, scale, *refs):
    z_refs, (w_ref, out_ref) = refs[:-2], refs[-2:]
    blocks = CHUNK * len(z_refs)
    group = LANES // blocks
    weight = w_ref[...] * scale
    flipped = jnp.where(low_half(weight.shape), weight, -weight)
    lane = lax.broadcasted_iota(jnp.int32, (blocks, LANES), 1)
    row = lax.broadcasted_iota(jnp.int32, (blocks, LANES), 0)
    upper = row <= lane % blocks

    def step(g, carry):
        left, real_side, imag_side = [], [], []
        for k in range(group):
            start = pl.multiple_of((g * group + k) * CHUNK, CHUNK)
            z = jnp.concatenate([ref[pl.ds(start, CHUNK), :] for ref in z_refs], axis=0)
            left.append(z)
            real_side.append(z * weight)
            imag_side.append(pltpu.roll(z, HALF, 1) * flipped)
        lh, ll = split(jnp.concatenate(left, axis=0))
        rh, rl = split(jnp.concatenate(real_side + imag_side, axis=0))
        full = lax.dot_general(
            jnp.concatenate([lh, ll, lh], axis=1),
            jnp.concatenate([rh, rh, rl], axis=1),
            (((1,), (1,)), ((), ())),
            preferred_element_type=F32,
        )
        real, imag = full[:blocks, :LANES], full[:blocks, LANES:]
        for k in range(1, group):
            here = lane // blocks == k
            rows = slice(k * blocks, (k + 1) * blocks)
            real = jnp.where(here, full[rows, :LANES], real)
            imag = jnp.where(here, full[rows, LANES:], imag)
        packed = jnp.where(upper, real, imag)
        parts = [packed[i * 8 : (i + 1) * 8] for i in range(group)]
        small = lane[:8]
        step_size = 1
        while step_size < group:
            span = step_size * blocks
            odd = (small // span) % 2 == 1
            fresh = list(parts)
            for i in range(group):
                if i & step_size == 0:
                    a, b = parts[i], parts[i + step_size]
                    fresh[i] = jnp.where(odd, pltpu.roll(b, span, 1), a)
                    fresh[i + step_size] = jnp.where(odd, b, pltpu.roll(a, LANES - span, 1))
            parts = fresh
            step_size *= 2
        for k in range(group):
            out_ref[g * group + k] = parts[k]
        return carry

    lax.fori_loop(0, tile // group, step, 0, unroll=2)


def gram(spectra, weights, slots, tile, total_points):
    blocks = CHUNK * len(spectra)
    rows = blocks * blocks // LANES
    return pl.pallas_call(
        functools.partial(gram_kernel, tile, 1.0 / total_points),
        grid=(slots // tile,),
        in_specs=[pl.BlockSpec((tile * CHUNK, LANES), lambda i: (i, 0))] * len(spectra)
        + [pl.BlockSpec((1, LANES), lambda i: (0, 0))],
        out_specs=pl.BlockSpec((tile, rows, LANES), lambda i: (i, 0, 0)),
        out_shape=jax.ShapeDtypeStruct((slots, rows, LANES), F32),
        compiler_params=params(48),
        name="gram",
    )(*spectra, weights)


def power_kernel(x_ref, out_ref):
    blocks, _, count = x_ref.shape
    x = x_ref[...]
    flip = jnp.swapaxes(x, 0, 1)
    b = lax.broadcasted_iota(jnp.int32, x.shape, 0)
    c = lax.broadcasted_iota(jnp.int32, x.shape, 1)
    real = jnp.where(b <= c, x, flip)
    imag = jnp.where(b < c, flip, jnp.where(b > c, -x, 0.0))

    def apply(vr, vi):
        vr, vi = vr[:, None, :], vi[:, None, :]
        return jnp.sum(real * vr - imag * vi, axis=0), jnp.sum(real * vi + imag * vr, axis=0)

    vr = jnp.full((blocks, count), 1.0 / math.sqrt(blocks), F32)
    vi = jnp.zeros((blocks, count), F32)
    for _ in range(POWER):
        ur, ui = apply(vr, vi)
        length = lax.rsqrt(jnp.sum(ur * ur + ui * ui, axis=0, keepdims=True) + 1e-06)
        vr, vi = ur * length, ui * length
    ur, ui = apply(vr, vi)
    energy = jnp.sum(vr * ur + vi * ui, axis=0, keepdims=True)
    out_ref[0:blocks, :] = vr
    out_ref[blocks : 2 * blocks, :] = vi
    out_ref[2 * blocks : 2 * blocks + 8, :] = jnp.broadcast_to(energy, (8, count))


def power(packed):
    blocks, _, count = packed.shape
    return pl.pallas_call(
        power_kernel,
        out_shape=jax.ShapeDtypeStruct((2 * blocks + 8, count), F32),
        compiler_params=params(32),
        name="power",
    )(packed)


def modes_kernel(slots, *refs):
    z_refs, (v_ref, order_ref, sign_ref, out_ref, energy_ref, s_ref) = refs[:-6], refs[-6:]
    blocks = CHUNK * len(z_refs)
    tile = 32

    def step(i, carry):
        start = pl.multiple_of(i * tile, tile)
        vec = v_ref[pl.ds(start, tile), :]
        real = jnp.zeros((tile, LANES), F32)
        imag = jnp.zeros((tile, LANES), F32)
        for n, ref in enumerate(z_refs):
            for j in range(CHUNK):
                b = n * CHUNK + j
                z = ref[pl.ds(start * CHUNK + j, tile, stride=CHUNK), :]
                real = real + z * vec[:, b : b + 1]
                imag = imag + z * vec[:, blocks + b : blocks + b + 1]
        turned = pltpu.roll(imag, HALF, 1)
        both = real + jnp.where(low_half(turned.shape), -turned, turned)
        energy = vec[:, 2 * blocks : 2 * blocks + 1]
        both = both * lax.rsqrt(energy + 1e-06)
        value = jnp.concatenate([both, jnp.broadcast_to(energy, (tile, LANES))], axis=1)
        for part in range(3):
            high = value.astype(BF16)
            s_ref[part, pl.ds(start, tile), :] = high
            value = value - high.astype(F32)
        return carry

    lax.fori_loop(0, slots // tile, step, 0)
    order = order_ref[...]
    total = jnp.dot(order, s_ref[0], preferred_element_type=F32)
    total = total + jnp.dot(order, s_ref[1], preferred_element_type=F32)
    total = total + jnp.dot(order, s_ref[2], preferred_element_type=F32)
    out_ref[...] = total[:, :LANES] * sign_ref[...]
    energy_ref[...] = total[:, LANES:]


def modes(spectra, vectors, order, sign, slots):
    total = order.shape[0]
    return pl.pallas_call(
        functools.partial(modes_kernel, slots),
        out_shape=[jax.ShapeDtypeStruct((total, LANES), F32)] * 2,
        scratch_shapes=[pltpu.VMEM((3, slots, 2 * LANES), BF16)],
        compiler_params=params(56),
        name="modes",
    )(*spectra, vectors, order, sign)


def place_kernel(x_ref, out_ref):
    low = low_half(x_ref.shape[1:])
    for i in range(x_ref.shape[0] // 2):
        first, second = x_ref[2 * i], x_ref[2 * i + 1]
        cols = slice(i * LANES, (i + 1) * LANES)
        out_ref[0, :, cols] = jnp.where(low, first, pltpu.roll(second, HALF, 1))
        out_ref[1, :, cols] = jnp.where(low, pltpu.roll(first, HALF, 1), second)


def place(pieces):
    count, rows, _ = pieces.shape
    return pl.pallas_call(
        place_kernel,
        out_shape=jax.ShapeDtypeStruct((2, rows, count * HALF), F32),
        compiler_params=params(32),
        name="place",
    )(pieces)


def exchange(value, axes):
    return lax.all_to_all(value, axes, 0, 0, tiled=True)


def body(mesh_shape, snapshots, quad_weights):
    tm_size, space_size = mesh_shape["tm"], mesh_shape["space"]
    local_times, blocks, points = snapshots.shape
    total_times = local_times * tm_size
    total_points = points * space_size
    devices = tm_size * space_size
    per_device = -(-(total_times // 2 + 1) // devices)
    slots = per_device * devices
    tile = slots // 4
    tables = transform_tables(total_times, slots, tile)

    spectra = []
    for chunk in range(blocks // CHUNK):
        packed = pack(snapshots, chunk, tm_size)
        columns = exchange(packed, "tm").reshape(total_times, CHUNK * HALF)
        spectra.append(transform(columns, tables, slots, tile))

    here = lax.axis_index("tm") * HALF
    weights = lax.dynamic_slice(quad_weights, (here,), (HALF,))
    weights = jnp.concatenate([weights, weights])[None, :]
    matrices = gram(spectra, weights, slots, tile, total_points)

    rows = matrices.shape[1]
    space = lax.axis_index("space")
    levels = space_size.bit_length() - 1
    part = matrices.reshape(tm_size, *[2] * levels, per_device, rows, LANES)
    for level in range(levels):
        axis = levels - level
        bit = space >> level & 1
        kept = lax.dynamic_index_in_dim(part, bit, axis, keepdims=False)
        given = lax.dynamic_index_in_dim(part, 1 - bit, axis, keepdims=False)
        pairs = [(i, i ^ (1 << level)) for i in range(space_size)]
        part = kept + lax.ppermute(given, "space", pairs)
    part = exchange(part, "tm").sum(axis=0)

    part = part.reshape(per_device, 8, LANES // blocks, blocks)
    part = part.transpose(2, 1, 3, 0).reshape(blocks, blocks, per_device)
    vectors = power(part).T
    vectors = jnp.pad(vectors, ((0, 0), (0, LANES - vectors.shape[1])))
    vectors = jnp.broadcast_to(vectors[None], (devices, per_device, LANES))
    vectors = exchange(vectors, ("tm", "space")).reshape(slots, LANES)

    order, sign = output_order(total_times, tm_size, slots)
    pieces, energies = modes(spectra, vectors, order, sign, slots)
    pieces = exchange(pieces.reshape(tm_size, local_times, LANES), "tm")
    energies = energies.reshape(tm_size, local_times, LANES)[:, :, 0]
    energies = lax.dynamic_index_in_dim(energies, lax.axis_index("tm"), 0, keepdims=False)
    return place(pieces), energies


def fits(mesh_shape, times, blocks, points):
    tm_size, space_size = mesh_shape["tm"], mesh_shape["space"]
    return (
        points == space_size * tm_size * HALF
        and tm_size % 2 == 0
        and space_size & (space_size - 1) == 0
        and times % (tm_size * 8) == 0
        and blocks % CHUNK == 0
        and blocks == 32
    )


def matvec(matrix, vector):
    return jnp.einsum("fbc,fc->fb", matrix, vector, precision=lax.Precision.HIGHEST)


def power_modes(real_gram, imag_gram):
    vec_real = jnp.ones(real_gram.shape[:2], jnp.float32) / math.sqrt(real_gram.shape[1])
    vec_imag = jnp.zeros(real_gram.shape[:2], jnp.float32)
    for sweep_idx in range(POWER):
        new_real = matvec(real_gram, vec_real) - matvec(imag_gram, vec_imag)
        new_imag = matvec(real_gram, vec_imag) + matvec(imag_gram, vec_real)
        length = lax.rsqrt(
            jnp.sum(new_real * new_real + new_imag * new_imag, axis=1, keepdims=True) + 1e-06
        )
        vec_real = new_real * length
        vec_imag = new_imag * length
    image_real = matvec(real_gram, vec_real) - matvec(imag_gram, vec_imag)
    image_imag = matvec(real_gram, vec_imag) + matvec(imag_gram, vec_real)
    energy = jnp.sum(vec_real * image_real + vec_imag * image_imag, axis=1)
    return (vec_real, vec_imag, energy)


def general_body(snapshots, quad_weights):
    tm_size = lax.axis_size("tm")
    bit_count = tm_size.bit_length() - 1
    local_times, blocks, points = snapshots.shape
    total_times = local_times * tm_size
    total_points = points * lax.axis_size("space")
    norm_factor = 1.0 / math.sqrt(0.375 * total_times)
    flattened = snapshots.reshape(local_times, blocks * points)
    columns = lax.all_to_all(flattened, "tm", split_axis=1, concat_axis=0, tiled=True)
    col_count = columns.shape[1]
    times_all = jnp.arange(total_times, dtype=jnp.int32)
    window = (
        0.5 - 0.5 * jnp.cos(2.0 * math.pi * times_all.astype(jnp.float32) / total_times)
    ) * norm_factor
    row_block = min(256, total_times)

    def one_block(block_idx):
        row_ids = block_idx * row_block + jnp.arange(row_block, dtype=jnp.int32)
        frequency = bit_reverse(row_ids // local_times, bit_count) + tm_size * (
            row_ids % local_times
        )
        angles = (
            -2.0
            * math.pi
            * (frequency[:, None] * times_all[None, :] % total_times).astype(jnp.float32)
            / total_times
        )
        cos_tab = jnp.cos(angles) * window[None, :]
        sin_tab = jnp.sin(angles) * window[None, :]
        return (
            jnp.dot(cos_tab, columns, precision=lax.Precision.HIGHEST),
            jnp.dot(sin_tab, columns, precision=lax.Precision.HIGHEST),
        )

    spec_real, spec_imag = lax.map(one_block, jnp.arange(total_times // row_block, dtype=jnp.int32))
    spectrum = jnp.stack(
        [spec_real.reshape(total_times, col_count), spec_imag.reshape(total_times, col_count)]
    )
    returned = lax.all_to_all(spectrum, "tm", split_axis=1, concat_axis=2, tiled=True)
    spectral = returned.reshape(2, local_times, blocks, points)
    weighted = spectral * quad_weights
    gram_full = (
        jnp.einsum("pfbx,qfcx->fpbqc", weighted, spectral, precision=lax.Precision.HIGHEST)
        / total_points
    )
    real_gram = gram_full[:, 0, :, 0] + gram_full[:, 1, :, 1]
    imag_gram = gram_full[:, 0, :, 1] - gram_full[:, 1, :, 0]
    real_gram, imag_gram = lax.psum((real_gram, imag_gram), "space")
    vec_real, vec_imag, energy = power_modes(real_gram, imag_gram)
    inverse_root = lax.rsqrt(energy + 1e-06)[:, None]
    modes_real = jnp.einsum(
        "fb,fbx->fx", vec_real, spectral[0], precision=lax.Precision.HIGHEST
    ) - jnp.einsum("fb,fbx->fx", vec_imag, spectral[1], precision=lax.Precision.HIGHEST)
    modes_imag = jnp.einsum(
        "fb,fbx->fx", vec_imag, spectral[0], precision=lax.Precision.HIGHEST
    ) + jnp.einsum("fb,fbx->fx", vec_real, spectral[1], precision=lax.Precision.HIGHEST)
    return (jnp.stack([modes_real * inverse_root, modes_imag * inverse_root]), energy)


def solution(mesh):
    shape = dict(mesh.shape)

    def program(snapshots, quad_weights):
        chosen = general_body
        if fits(shape, *snapshots.shape):
            chosen = functools.partial(body, shape)
        return jax.shard_map(
            chosen,
            mesh=mesh,
            in_specs=(P("tm", None, "space"), P("space")),
            out_specs=(P(None, "tm", "space"), P("tm")),
            check_vma=False,
        )(snapshots, quad_weights)

    return program
```

```python
import functools
import math

import jax
import jax.numpy as jnp
import ml_dtypes
import numpy as np
from jax import lax
from jax.experimental import pallas as pl
from jax.experimental.pallas import tpu as pltpu
from jax.sharding import PartitionSpec as P

POWER = 3
CHUNK = 8
HALF = 64
LANES = 128
BF16 = jnp.bfloat16
F32 = jnp.float32


def bit_reverse(value, bit_count):
    return sum((value >> i & 1) << (bit_count - 1 - i) for i in range(bit_count))


def split_np(table):
    high = table.astype(ml_dtypes.bfloat16)
    low = (table - high.astype(np.float64)).astype(ml_dtypes.bfloat16)
    return high, low


def split(value):
    high = value.astype(BF16)
    return high, (value - high.astype(F32)).astype(BF16)


def low_half(shape):
    return lax.broadcasted_iota(jnp.int32, shape, len(shape) - 1) < HALF


def in_hbm(arrays):
    return [pltpu.with_memory_space_constraint(array, pltpu.HBM) for array in arrays]


def params(mib):
    return pltpu.CompilerParams(vmem_limit_bytes=mib * 2**20)


def slot_of(freq, total_times):
    part = total_times // 8
    return (freq - 1) % 4 * part + freq // 4


@functools.lru_cache(None)
def transform_tables(total_times, slots):
    part, quarter = total_times // 8, total_times // 4
    t = np.arange(quarter)

    def waves(rest, count):
        k = 4 * np.arange(count) + rest
        phase = 2 * np.pi * (k[:, None] * t[None, :] % total_times) / total_times
        live = (k <= total_times // 2)[:, None]
        return np.cos(phase) * live, np.sin(phase) * live

    c, s = waves(1, part)
    ones = np.block([[c, -s], [-s, -c]])
    c, s = waves(3, part)
    threes = np.block([[c, s], [-s, c]])
    c, s = waves(2, part)
    twos = np.concatenate([c, -s])
    c, s = waves(0, slots - 3 * part)
    fours = np.concatenate([c, -s])
    odd = split_np(np.concatenate([ones, threes]))
    return (*odd, *split_np(twos), *split_np(fours))


@functools.lru_cache(None)
def window_table(total_times):
    t = np.arange(total_times)
    window = (0.5 - 0.5 * np.cos(2 * np.pi * t / total_times)) / math.sqrt(0.375 * total_times)
    return np.broadcast_to(window[:, None], (total_times, LANES)).astype(np.float32)


def pack_kernel(offsets, *refs):
    x_refs, out_refs = refs[: len(offsets)], refs[-len(offsets) :]
    window = refs[len(offsets)][...]
    times = window.shape[0]
    low = low_half((times, LANES))
    me = lax.axis_index("tm")
    for m, x_ref, out_ref in zip(offsets, x_refs, out_refs):
        rows = x_ref.reshape(times * CHUNK, LANES)
        even = (m ^ me) % 2 == 0
        for j in range(CHUNK // 2):
            first = rows[pl.ds(j, times, stride=CHUNK), :] * window
            second = rows[pl.ds(j + CHUNK // 2, times, stride=CHUNK), :] * window
            left = jnp.where(low, first, pltpu.roll(second, HALF, 1))
            right = jnp.where(low, pltpu.roll(first, HALF, 1), second)
            out_ref[:, j * LANES : (j + 1) * LANES] = jnp.where(even, left, right)


def pack(snapshots, window, chunks, offsets, after):
    times = snapshots.shape[0]
    width = CHUNK * HALF

    def tile_spec(m):
        place = lambda n: (0, chunks[0] + n, m // 2 ^ lax.axis_index("tm") // 2)
        return pl.BlockSpec((times, CHUNK, LANES), place)

    return pl.pallas_call(
        functools.partial(pack_kernel, offsets),
        grid=(len(chunks),),
        in_specs=[tile_spec(m) for m in offsets]
        + [pl.BlockSpec((times, LANES), lambda _: (lax.axis_index("tm"), 0))]
        + [pl.BlockSpec(memory_space=pl.ANY)] * len(after),
        out_specs=[pl.BlockSpec((None, times, width), lambda n: (n, 0, 0))] * len(offsets),
        out_shape=[pltpu.HBM((len(chunks), times, width), F32)] * len(offsets),
        compiler_params=params(24),
        name="pack",
    )(*in_hbm([snapshots] * len(offsets)), window, *in_hbm(after))


def transform_kernel(*refs):
    odd_high, odd_low, two_high, two_low, four_high, four_low = refs[:6]
    piece_refs, (out_ref, x_ref, odd_ref, two_ref, four_ref) = refs[6:-5], refs[-5:]
    me = lax.axis_index("tm")
    for m, piece_ref in enumerate(piece_refs):
        times = piece_ref.shape[0]
        rows = pl.ds(pl.multiple_of((me ^ m) * times, times), times)
        x_ref[rows, :] = piece_ref[...]
    total, width = x_ref.shape
    quarter, part = total // 4, total // 8

    def keep(ref, rows, cols, value):
        ref[0, rows, cols], ref[1, rows, cols] = split(value)

    for first in range(0, quarter, part):
        for j in range(width // LANES):
            cols = slice(j * LANES, (j + 1) * LANES)
            rows = slice(first, first + part)
            x = [x_ref[n * quarter + first : n * quarter + first + part, cols] for n in range(4)]
            keep(odd_ref, rows, cols, x[0] - x[2])
            keep(odd_ref, slice(quarter + first, quarter + first + part), cols, x[1] - x[3])
            left, right = x[0] + x[2], x[1] + x[3]
            keep(two_ref, rows, cols, left - right)
            keep(four_ref, rows, cols, left + right)

    dot = functools.partial(jnp.dot, preferred_element_type=F32)

    def product(high, low, values):
        return dot(high, values[0]) + dot(high, values[1]) + dot(low, values[0])

    def store(start, both):
        count = both.shape[0] // 2
        low = low_half((count, LANES))
        for j in range(CHUNK // 2):
            cols = slice(j * LANES, (j + 1) * LANES)
            real, imag = both[:count, cols], both[count:, cols]
            first = jnp.where(low, real, pltpu.roll(imag, HALF, 1))
            second = jnp.where(low, pltpu.roll(real, HALF, 1), imag)
            for b, value in ((j, first), (j + CHUNK // 2, second)):
                out_ref[pl.ds(start * CHUNK + b, count, stride=CHUNK), :] = value

    for n in range(2):
        rows = slice(2 * n * part, 2 * (n + 1) * part)
        store(2 * n * part, product(odd_high[rows, :], odd_low[rows, :], odd_ref))
    store(part, product(two_high[...], two_low[...], two_ref))
    store(3 * part, product(four_high[...], four_low[...], four_ref))


def transform(pieces, tables, slots):
    chunks, times, width = pieces[0].shape
    total = times * len(pieces)
    quarter = total // 4
    return pl.pallas_call(
        transform_kernel,
        grid=(chunks,),
        in_specs=[pl.BlockSpec(table.shape, lambda n: (0, 0)) for table in tables]
        + [pl.BlockSpec((None, times, width), lambda n: (n, 0, 0))] * len(pieces),
        out_specs=pl.BlockSpec((None, slots * CHUNK, LANES), lambda n: (n, 0, 0)),
        out_shape=pltpu.HBM((chunks, slots * CHUNK, LANES), F32),
        scratch_shapes=[
            pltpu.VMEM((total, width), F32),
            pltpu.VMEM((2, 2 * quarter, width), BF16),
            pltpu.VMEM((2, quarter, width), BF16),
            pltpu.VMEM((2, quarter, width), BF16),
        ],
        compiler_params=params(40),
        name="transform",
    )(*tables, *in_hbm(pieces))


def first_lane(chunk, chunks):
    return sum(16 * i + 8 for i in range(chunk + 1, chunks))


GROUP = 8


def chunk_tiles(chunk, chunks, weight, parts, before):
    flipped = jnp.where(low_half(weight.shape), weight, -weight)
    width = CHUNK * (chunk + 1)
    stride = width if LANES % width == 0 else 32
    left, right = [], []
    for row in parts:
        row = row[: chunk + 1]
        right.extend((row + row[-1:])[: stride // CHUNK])
        left.append(row[-1] * weight)
        left.append(pltpu.roll(row[-1], HALF, 1) * flipped)
    lh, ll = split(jnp.concatenate(left, axis=0))
    rh, rl = split(jnp.concatenate(right, axis=0))
    full = lax.dot_general(
        jnp.concatenate([lh, ll, lh], axis=1),
        jnp.concatenate([rh, rh, rl], axis=1),
        (((1,), (1,)), ((), ())),
        preferred_element_type=F32,
    )
    if full.shape[1] < LANES:
        full = jnp.concatenate([full] * (LANES // full.shape[1]), axis=1)
    start = first_lane(chunk, chunks)
    row = lax.broadcasted_iota(jnp.int32, (CHUNK, LANES), 0)
    own = lax.broadcasted_iota(jnp.int32, (CHUNK, LANES), 1) - start
    past = own >= width
    corner = (own >= width - CHUNK) & (own < width) & (own - (width - CHUNK) > row)
    valid = (own >= 0) & (own < width + CHUNK * chunk)
    tiles = []
    for k in range(GROUP):
        first = k * stride // LANES * LANES
        real = full[16 * k : 16 * k + 8, first : first + LANES]
        imag = full[16 * k + 8 : 16 * k + 16, first : first + LANES]
        shift = (start - (k * stride - first)) % LANES
        out = pltpu.roll(real, shift, 1)
        out = jnp.where(corner, pltpu.roll(imag, shift, 1), out)
        out = jnp.where(past, pltpu.roll(imag, (shift + width) % LANES, 1), out)
        tiles.append(jnp.where(valid, out, before[k]))
    return tiles


def early_gram_kernel(tile, chunks, scale, z_ref, w_ref, out_ref):
    weight = w_ref[...] * scale

    def step(g, carry):
        parts = []
        for k in range(GROUP):
            rows = pl.ds(pl.multiple_of((g * GROUP + k) * CHUNK, CHUNK), CHUNK)
            parts.append([z_ref[n, rows, :] for n in range(chunks - 1)])
        tiles = [jnp.zeros((CHUNK, LANES), F32)] * GROUP
        for chunk in range(chunks - 1):
            tiles = chunk_tiles(chunk, chunks, weight, parts, tiles)
        for k in range(GROUP):
            out_ref[g * GROUP + k] = tiles[k]
        return carry

    lax.fori_loop(0, tile // GROUP, step, 0, unroll=True)


def early_gram(spectra, weights, slots, tile, total_points):
    chunks = spectra.shape[0] + 1
    return pl.pallas_call(
        functools.partial(early_gram_kernel, tile, chunks, 1.0 / total_points),
        grid=(slots // tile,),
        in_specs=[
            pl.BlockSpec((chunks - 1, tile * CHUNK, LANES), lambda i: (0, i, 0)),
            pl.BlockSpec((1, LANES), lambda i: (0, 0)),
        ],
        out_specs=pl.BlockSpec((tile, 8, LANES), lambda i: (i, 0, 0)),
        out_shape=pltpu.HBM((slots, 8, LANES), F32),
        compiler_params=params(24),
        name="early_gram",
    )(*in_hbm([spectra]), weights)


def late_gram_kernel(tile, half, scale, *refs):
    sources, w_ref, out_ref = refs[:3], refs[3], refs[4]
    (early_ref, late_ref, before_ref), sems = refs[5:8], refs[8]
    chunks = early_ref.shape[0] + 1
    weight = w_ref[...] * scale
    count = out_ref.shape[0]
    base = pl.multiple_of((lax.axis_index("space") % 2 ^ half) * count, GROUP)

    def copies(t):
        there = pl.ds(pl.multiple_of((base + t * tile) * CHUNK, 8), tile * CHUNK)
        here = pl.ds(pl.multiple_of(t * tile * CHUNK, 8), tile * CHUNK)
        there_tile = pl.ds(pl.multiple_of(base + t * tile, 8), tile)
        here_tile = pl.ds(pl.multiple_of(t * tile, 8), tile)
        return [
            pltpu.make_async_copy(sources[0].at[:, there], early_ref.at[:, here], sems.at[0, t]),
            pltpu.make_async_copy(sources[1].at[:, there], late_ref.at[:, here], sems.at[1, t]),
            pltpu.make_async_copy(
                sources[2].at[there_tile], before_ref.at[here_tile], sems.at[2, t]
            ),
        ]

    for t in range(count // tile):
        for copy in copies(t):
            copy.start()

    def step(g, carry):
        parts, before = [], []
        for k in range(GROUP):
            rows = pl.ds(pl.multiple_of((g * GROUP + k) * CHUNK, CHUNK), CHUNK)
            parts.append([early_ref[n, rows, :] for n in range(chunks - 1)])
            parts[-1].append(late_ref[0, rows, :])
            before.append(before_ref[g * GROUP + k])
        tiles = chunk_tiles(chunks - 1, chunks, weight, parts, before)
        for k in range(GROUP):
            out_ref[g * GROUP + k] = tiles[k]
        return carry

    groups = tile // GROUP

    def one_tile(t, carry):
        for copy in copies(t):
            copy.wait()
        return lax.fori_loop(0, groups, lambda g, c: step(t * groups + g, c), carry, unroll=True)

    lax.fori_loop(0, count // tile, one_tile, 0)


def late_gram(early, late, weights, before, slots, tile, total_points, half):
    count = slots // 2
    sizes = [(z.shape[0], count * CHUNK, LANES) for z in (early, late)] + [(count, 8, LANES)]
    return pl.pallas_call(
        functools.partial(late_gram_kernel, tile, half, 1.0 / total_points),
        in_specs=[pl.BlockSpec(memory_space=pl.ANY)] * 3
        + [pl.BlockSpec(memory_space=pltpu.VMEM)],
        out_shape=pltpu.HBM((count, 8, LANES), F32),
        scratch_shapes=[pltpu.VMEM(size, F32) for size in sizes]
        + [pltpu.SemaphoreType.DMA((3, count // tile))],
        compiler_params=params(24),
        name="late_gram",
    )(*in_hbm([early, late, before]), weights)


def power_kernel(blocks, x_ref, out_ref):
    count = x_ref.shape[2]
    chunks = blocks // CHUNK
    real = [[None] * chunks for _ in range(chunks)]
    imag = [[None] * chunks for _ in range(chunks)]
    for c in range(chunks):
        start = first_lane(c, chunks)
        for d in range(c):
            x = x_ref[start + CHUNK * d : start + CHUNK * (d + 1)]
            y = x_ref[start + CHUNK * (c + 1 + d) : start + CHUNK * (c + 2 + d)]
            real[d][c], real[c][d] = x, jnp.swapaxes(x, 0, 1)
            imag[d][c], imag[c][d] = y, -jnp.swapaxes(y, 0, 1)
        x = x_ref[start + CHUNK * c : start + CHUNK * (c + 1)]
        flip = jnp.swapaxes(x, 0, 1)
        b = lax.broadcasted_iota(jnp.int32, x.shape, 0)
        s = lax.broadcasted_iota(jnp.int32, x.shape, 1)
        real[c][c] = jnp.where(b <= s, x, flip)
        imag[c][c] = jnp.where(b > s, x, jnp.where(b < s, -flip, 0.0))
    whole = lambda m: jnp.concatenate([jnp.concatenate(r, axis=1) for r in m], axis=0)
    real, imag = whole(real), -whole(imag)

    def apply(vr, vi):
        vr, vi = vr[:, None, :], vi[:, None, :]
        return jnp.sum(real * vr - imag * vi, axis=0), jnp.sum(real * vi + imag * vr, axis=0)

    vr = jnp.full((blocks, count), 1.0 / math.sqrt(blocks), F32)
    vi = jnp.zeros((blocks, count), F32)
    for _ in range(POWER):
        ur, ui = apply(vr, vi)
        length = lax.rsqrt(jnp.sum(ur * ur + ui * ui, axis=0, keepdims=True) + 1e-06)
        vr, vi = ur * length, ui * length
    ur, ui = apply(vr, vi)
    energy = jnp.sum(vr * ur + vi * ui, axis=0, keepdims=True)
    out_ref[0:blocks, :] = vr
    out_ref[blocks : 2 * blocks, :] = vi
    out_ref[2 * blocks : 2 * blocks + 8, :] = jnp.broadcast_to(energy, (8, count))


def power(packed, blocks):
    return pl.pallas_call(
        functools.partial(power_kernel, blocks),
        out_shape=jax.ShapeDtypeStruct((2 * blocks + 8, packed.shape[2]), F32),
        compiler_params=params(32),
        name="power",
    )(packed)


def reverse_rows(value):
    row = lax.broadcasted_iota(jnp.int32, (8, LANES), 0)
    tiles = []
    for start in range(0, value.shape[0], 8):
        tile = value[start : start + 8]
        for span in (1, 2, 4):
            upper = (row & span) == 0
            tile = jnp.where(upper, pltpu.roll(tile, 8 - span, 0), pltpu.roll(tile, span, 0))
        tiles.append(tile)
    return jnp.concatenate(tiles[::-1], axis=0)


def modes_kernel(tile, classes, total_times, *refs):
    early, late, v_ref, out_ref, energy_ref, z_ref, s_ref, e_ref, sems = refs
    chunks = z_ref.shape[0]
    blocks = CHUNK * z_ref.shape[0]
    group = 8
    lane = lax.broadcasted_iota(jnp.int32, (group, LANES), 1)
    row = lax.broadcasted_iota(jnp.int32, (group, LANES), 0)
    per_tile = LANES // blocks
    low = low_half((group, LANES))

    def spread(vector):
        vector = jnp.where(lane < blocks, vector, 0.0)
        span = blocks
        while span < LANES:
            vector = vector + pltpu.roll(vector, span, 1)
            span *= 2
        parts = []
        for first in range(0, group, per_tile):
            parts.append(jnp.where(lane // blocks + first == row, vector, 0.0))
        return jnp.concatenate(parts, axis=1)

    def step(g, carry):
        start = pl.multiple_of(g * group, group)
        vec = v_ref[pl.ds(start, group), :]
        both = jnp.concatenate([spread(vec), spread(pltpu.roll(vec, LANES - blocks, 1))], axis=0)
        vh, vl = split(both)
        z = []
        for k in range(group):
            rows = pl.ds(pl.multiple_of((g * group + k) * CHUNK, CHUNK), CHUNK)
            z.append(z_ref[:, rows, :].reshape(blocks, LANES))
        zh, zl = split(jnp.concatenate(z, axis=0))
        full = jnp.dot(
            jnp.concatenate([vh, vl], axis=0),
            jnp.concatenate([zh, zl], axis=1),
            preferred_element_type=F32,
        )
        sums = full[:16, :LANES] + full[:16, LANES:] + full[16:, :LANES]
        turned = pltpu.roll(sums[8:], HALF, 1)
        value = sums[:8] + jnp.where(low, -turned, turned)
        energy = jnp.broadcast_to(vec[:, 2 * blocks : 2 * blocks + 1], (group, LANES))
        s_ref[pl.ds(start, group), :] = value * lax.rsqrt(energy + 1e-06)
        e_ref[pl.ds(start, group), :] = energy
        return carry

    groups = tile // group
    tiles = v_ref.shape[0] // tile

    def copies(t):
        rows = pl.ds(pl.multiple_of(t * tile * CHUNK, CHUNK), tile * CHUNK)
        first, second = z_ref.at[: chunks - 1, rows], z_ref.at[chunks - 1 :, rows]
        return (
            pltpu.make_async_copy(early.at[:, rows], first, sems.at[0, t]),
            pltpu.make_async_copy(late.at[:, rows], second, sems.at[1, t]),
        )

    for t in range(tiles):
        for copy in copies(t):
            copy.start()

    def one_tile(t, carry):
        for copy in copies(t):
            copy.wait()
        return lax.fori_loop(0, groups, lambda g, c: step(t * groups + g, c), carry, unroll=True)

    lax.fori_loop(0, tiles, one_tile, 0)

    half = out_ref.shape[0] // classes // 2
    bits = classes.bit_length() - 1
    low = low_half((half, LANES))
    for d in range(classes):
        r = bit_reverse(d, bits)
        direct = pl.ds(slot_of(r, total_times), half, stride=classes // 4)
        mirror = pl.ds(slot_of(classes - r, total_times), half, stride=classes // 4)
        start = 2 * half * d
        out_ref[start : start + half, :] = s_ref[direct, :]
        energy_ref[start : start + half, :] = e_ref[direct, :]
        turned = reverse_rows(s_ref[mirror, :])
        out_ref[start + half : start + 2 * half, :] = jnp.where(low, turned, -turned)
        energy_ref[start + half : start + 2 * half, :] = reverse_rows(e_ref[mirror, :])


def modes(early, late, vectors, total, classes, slots, tile):
    return pl.pallas_call(
        functools.partial(modes_kernel, tile, classes, total),
        in_specs=[
            pl.BlockSpec(memory_space=pl.ANY),
            pl.BlockSpec(memory_space=pl.ANY),
            pl.BlockSpec(memory_space=pltpu.VMEM),
        ],
        out_shape=[jax.ShapeDtypeStruct((total, LANES), F32)] * 2,
        scratch_shapes=[
            pltpu.VMEM((early.shape[0] + 1, *early.shape[1:]), F32),
            pltpu.VMEM((slots, LANES), F32),
            pltpu.VMEM((slots, LANES), F32),
            pltpu.SemaphoreType.DMA((2, slots // tile)),
        ],
        compiler_params=params(24),
        name="modes",
    )(*in_hbm([early, late]), vectors)


def place_kernel(x_ref, out_ref):
    low = low_half(x_ref.shape[1:])
    for i in range(x_ref.shape[0] // 2):
        first, second = x_ref[2 * i], x_ref[2 * i + 1]
        cols = slice(i * LANES, (i + 1) * LANES)
        out_ref[0, :, cols] = jnp.where(low, first, pltpu.roll(second, HALF, 1))
        out_ref[1, :, cols] = jnp.where(low, pltpu.roll(first, HALF, 1), second)


def place(pieces):
    count, rows, _ = pieces.shape
    return pl.pallas_call(
        place_kernel,
        out_shape=jax.ShapeDtypeStruct((2, rows, count * HALF), F32),
        compiler_params=params(32),
        name="place",
    )(pieces)


def exchange(value, axes):
    return lax.all_to_all(value, axes, 0, 0, tiled=True)


def body(mesh_shape, snapshots, quad_weights):
    tm_size, space_size = mesh_shape["tm"], mesh_shape["space"]
    local_times, blocks, points = snapshots.shape
    total_times = local_times * tm_size
    total_points = points * space_size
    devices = tm_size * space_size
    per_device = -(-(total_times // 2 + 1) // devices)
    slots = per_device * devices
    tile = slots // 4
    tables = transform_tables(total_times, slots)
    window = window_table(total_times)

    here = lax.axis_index("tm") * HALF
    weights = lax.dynamic_slice(quad_weights, (here,), (HALF,))
    weights = jnp.concatenate([weights, weights])[None, :]

    chunks = blocks // CHUNK

    def send(group, offsets, after):
        sent = dict(zip(offsets, pack(snapshots, window, group, tuple(offsets), after)))
        flying = {}
        for m, part in sent.items():
            pairs = [(d, d ^ m) for d in range(tm_size)]
            flying[m] = lax.ppermute(part, "tm", pairs) if m else part
        return sent, flying

    half, quarter = tm_size // 2, tm_size // 4
    first = [*range(half, half + quarter), *range(quarter)]
    second = [*range(half + quarter, tm_size), *range(quarter, half)]
    group = range(chunks - 1)
    sent, pieces = send(group, first, [])
    pieces |= send(group, second, [sent[0]])[1]
    group = range(chunks - 1, chunks)
    sent, last = send(group, first, [pieces[half]])
    last |= send(group, second, [sent[0], pieces[half + quarter]])[1]
    ordered = lambda pieces: [pieces[m] for m in range(tm_size)]
    early = transform(ordered(pieces), tables, slots)
    matrices = early_gram(early, weights, slots, tile, total_points)
    late = transform(ordered(last), tables, slots)

    space = lax.axis_index("space")

    def swap(value, level):
        pairs = [(i, i ^ (1 << level)) for i in range(space_size)]
        return lax.ppermute(value, "space", pairs)

    arriving = swap(late_gram(early, late, weights, matrices, slots, tile, total_points, 1), 0)
    part = late_gram(early, late, weights, matrices, slots, tile, total_points, 0)
    levels = space_size.bit_length() - 1
    shape = (*[2] * (levels - 1), tm_size, per_device, *part.shape[1:])
    part, arriving = part.reshape(shape), arriving.reshape(shape)
    for level in range(1, levels):
        bit = space >> level & 1
        pick = lambda value, i: lax.dynamic_index_in_dim(value, i, 0, keepdims=False)
        given = pick(part, 1 - bit) + pick(arriving, 1 - bit)
        part = pick(part, bit) + pick(arriving, bit)
        arriving = swap(given, level)
    part = exchange(part + arriving, "tm").sum(axis=0)

    vectors = power(part.transpose(2, 1, 0), blocks).T
    vectors = jnp.pad(vectors, ((0, 0), (0, LANES - vectors.shape[1])))
    vectors = jnp.broadcast_to(vectors[None], (devices, per_device, LANES))
    vectors = exchange(vectors, ("tm", "space"))
    vectors = vectors.reshape(tm_size, *[2] * levels, per_device, LANES)
    vectors = vectors.transpose(*range(levels, -1, -1), levels + 1, levels + 2)
    vectors = vectors.reshape(slots, LANES)

    pieces, energies = modes(early, late, vectors, total_times, tm_size, slots, tile)
    pieces = exchange(pieces.reshape(tm_size, local_times, LANES), "tm")
    energies = energies.reshape(tm_size, local_times, LANES)[:, :, 0]
    energies = lax.dynamic_index_in_dim(energies, lax.axis_index("tm"), 0, keepdims=False)
    return place(pieces), energies


def fits(mesh_shape, times, blocks, points):
    tm_size, space_size = mesh_shape["tm"], mesh_shape["space"]
    return (
        points == space_size * tm_size * HALF
        and tm_size == 8
        and space_size & (space_size - 1) == 0
        and times % (tm_size * 8) == 0
        and blocks % CHUNK == 0
        and blocks == 32
    )


def matvec(matrix, vector):
    return jnp.einsum("fbc,fc->fb", matrix, vector, precision=lax.Precision.HIGHEST)


def power_modes(real_gram, imag_gram):
    vec_real = jnp.ones(real_gram.shape[:2], jnp.float32) / math.sqrt(real_gram.shape[1])
    vec_imag = jnp.zeros(real_gram.shape[:2], jnp.float32)
    for sweep_idx in range(POWER):
        new_real = matvec(real_gram, vec_real) - matvec(imag_gram, vec_imag)
        new_imag = matvec(real_gram, vec_imag) + matvec(imag_gram, vec_real)
        length = lax.rsqrt(
            jnp.sum(new_real * new_real + new_imag * new_imag, axis=1, keepdims=True) + 1e-06
        )
        vec_real = new_real * length
        vec_imag = new_imag * length
    image_real = matvec(real_gram, vec_real) - matvec(imag_gram, vec_imag)
    image_imag = matvec(real_gram, vec_imag) + matvec(imag_gram, vec_real)
    energy = jnp.sum(vec_real * image_real + vec_imag * image_imag, axis=1)
    return (vec_real, vec_imag, energy)


def general_body(snapshots, quad_weights):
    tm_size = lax.axis_size("tm")
    bit_count = tm_size.bit_length() - 1
    local_times, blocks, points = snapshots.shape
    total_times = local_times * tm_size
    total_points = points * lax.axis_size("space")
    norm_factor = 1.0 / math.sqrt(0.375 * total_times)
    flattened = snapshots.reshape(local_times, blocks * points)
    columns = lax.all_to_all(flattened, "tm", split_axis=1, concat_axis=0, tiled=True)
    col_count = columns.shape[1]
    times_all = jnp.arange(total_times, dtype=jnp.int32)
    window = (
        0.5 - 0.5 * jnp.cos(2.0 * math.pi * times_all.astype(jnp.float32) / total_times)
    ) * norm_factor
    row_block = min(256, total_times)

    def one_block(block_idx):
        row_ids = block_idx * row_block + jnp.arange(row_block, dtype=jnp.int32)
        frequency = bit_reverse(row_ids // local_times, bit_count) + tm_size * (
            row_ids % local_times
        )
        angles = (
            -2.0
            * math.pi
            * (frequency[:, None] * times_all[None, :] % total_times).astype(jnp.float32)
            / total_times
        )
        cos_tab = jnp.cos(angles) * window[None, :]
        sin_tab = jnp.sin(angles) * window[None, :]
        return (
            jnp.dot(cos_tab, columns, precision=lax.Precision.HIGHEST),
            jnp.dot(sin_tab, columns, precision=lax.Precision.HIGHEST),
        )

    spec_real, spec_imag = lax.map(one_block, jnp.arange(total_times // row_block, dtype=jnp.int32))
    spectrum = jnp.stack(
        [spec_real.reshape(total_times, col_count), spec_imag.reshape(total_times, col_count)]
    )
    returned = lax.all_to_all(spectrum, "tm", split_axis=1, concat_axis=2, tiled=True)
    spectral = returned.reshape(2, local_times, blocks, points)
    weighted = spectral * quad_weights
    gram_full = (
        jnp.einsum("pfbx,qfcx->fpbqc", weighted, spectral, precision=lax.Precision.HIGHEST)
        / total_points
    )
    real_gram = gram_full[:, 0, :, 0] + gram_full[:, 1, :, 1]
    imag_gram = gram_full[:, 0, :, 1] - gram_full[:, 1, :, 0]
    real_gram, imag_gram = lax.psum((real_gram, imag_gram), "space")
    vec_real, vec_imag, energy = power_modes(real_gram, imag_gram)
    inverse_root = lax.rsqrt(energy + 1e-06)[:, None]
    modes_real = jnp.einsum(
        "fb,fbx->fx", vec_real, spectral[0], precision=lax.Precision.HIGHEST
    ) - jnp.einsum("fb,fbx->fx", vec_imag, spectral[1], precision=lax.Precision.HIGHEST)
    modes_imag = jnp.einsum(
        "fb,fbx->fx", vec_imag, spectral[0], precision=lax.Precision.HIGHEST
    ) + jnp.einsum("fb,fbx->fx", vec_real, spectral[1], precision=lax.Precision.HIGHEST)
    return (jnp.stack([modes_real * inverse_root, modes_imag * inverse_root]), energy)


def solution(mesh):
    shape = dict(mesh.shape)

    def program(snapshots, quad_weights):
        chosen = general_body
        if fits(shape, *snapshots.shape):
            chosen = functools.partial(body, shape)
        return jax.shard_map(
            chosen,
            mesh=mesh,
            in_specs=(P("tm", None, "space"), P("space")),
            out_specs=(P(None, "tm", "space"), P("tm")),
            check_vma=False,
        )(snapshots, quad_weights)

    return program
```

```python
import functools
import math

import jax
import jax.numpy as jnp
import ml_dtypes
import numpy as np
from jax import lax
from jax.experimental import pallas as pl
from jax.experimental.pallas import tpu as pltpu
from jax.sharding import PartitionSpec as P

POWER = 3
CHUNK = 8
HALF = 64
LANES = 128
BF16 = jnp.bfloat16
F32 = jnp.float32


def bit_reverse(value, bit_count):
    return sum((value >> i & 1) << (bit_count - 1 - i) for i in range(bit_count))


def split_np(table):
    high = table.astype(ml_dtypes.bfloat16)
    low = (table - high.astype(np.float64)).astype(ml_dtypes.bfloat16)
    return high, low


def split(value):
    high = value.astype(BF16)
    return high, (value - high.astype(F32)).astype(BF16)


def low_half(shape):
    return lax.broadcasted_iota(jnp.int32, shape, len(shape) - 1) < HALF


def in_hbm(arrays):
    return [pltpu.with_memory_space_constraint(array, pltpu.HBM) for array in arrays]


def params(mib):
    return pltpu.CompilerParams(vmem_limit_bytes=mib * 2**20)


def slot_of(freq, total_times):
    part = total_times // 8
    return (freq - 1) % 4 * part + freq // 4


@functools.lru_cache(None)
def transform_tables(total_times, slots):
    part, quarter = total_times // 8, total_times // 4
    t = np.arange(quarter)

    def waves(rest, count):
        k = 4 * np.arange(count) + rest
        phase = 2 * np.pi * (k[:, None] * t[None, :] % total_times) / total_times
        live = (k <= total_times // 2)[:, None]
        return np.cos(phase) * live, np.sin(phase) * live

    c, s = waves(1, part)
    ones = np.block([[c, -s], [-s, -c]])
    c, s = waves(3, part)
    threes = np.block([[c, s], [-s, c]])
    c, s = waves(2, part)
    twos = np.concatenate([c, -s])
    c, s = waves(0, slots - 3 * part)
    fours = np.concatenate([c, -s])
    odd = split_np(np.concatenate([ones, threes]))
    return (*odd, *split_np(twos), *split_np(fours))


@functools.lru_cache(None)
def window_table(total_times):
    t = np.arange(total_times)
    window = (0.5 - 0.5 * np.cos(2 * np.pi * t / total_times)) / math.sqrt(0.375 * total_times)
    return np.broadcast_to(window[:, None], (total_times, LANES)).astype(np.float32)


def pack_kernel(offsets, *refs):
    x_refs, out_refs = refs[: len(offsets)], refs[-len(offsets) :]
    window = refs[len(offsets)][...]
    times = window.shape[0]
    low = low_half((times, LANES))
    me = lax.axis_index("tm")
    for m, x_ref, out_ref in zip(offsets, x_refs, out_refs):
        blocks = x_ref.shape[1]
        rows = x_ref.reshape(times * blocks, LANES)
        even = (m ^ me) % 2 == 0
        for n in range(out_ref.shape[0]):
            for j in range(CHUNK // 2):
                b = n * CHUNK + j
                first = rows[pl.ds(b, times, stride=blocks), :] * window
                second = rows[pl.ds(b + CHUNK // 2, times, stride=blocks), :] * window
                left = jnp.where(low, first, pltpu.roll(second, HALF, 1))
                right = jnp.where(low, pltpu.roll(first, HALF, 1), second)
                out_ref[n, :, j * LANES : (j + 1) * LANES] = jnp.where(even, left, right)


def pack(snapshots, window, chunks, offsets, after):
    times = snapshots.shape[0]
    count, width = len(chunks), CHUNK * HALF

    def tile_spec(m):
        place = lambda _: (0, chunks[0] // count, m // 2 ^ lax.axis_index("tm") // 2)
        return pl.BlockSpec((times, CHUNK * count, LANES), place)

    return pl.pallas_call(
        functools.partial(pack_kernel, offsets),
        grid=(1,),
        in_specs=[tile_spec(m) for m in offsets]
        + [pl.BlockSpec((times, LANES), lambda _: (lax.axis_index("tm"), 0))]
        + [pl.BlockSpec(memory_space=pl.ANY)] * len(after),
        out_specs=[pl.BlockSpec((count, times, width), lambda _: (0, 0, 0))] * len(offsets),
        out_shape=[pltpu.HBM((count, times, width), F32)] * len(offsets),
        compiler_params=params(40),
        name="pack",
    )(*in_hbm([snapshots] * len(offsets) + [window, *after]))


def transform_columns(tables, x_ref, odd_ref, two_ref, four_ref, out_ref):
    odd_high, odd_low, two_high, two_low, four_high, four_low = tables
    total, width = x_ref.shape
    quarter, part = total // 4, total // 8

    def keep(ref, rows, cols, value):
        ref[0, rows, cols], ref[1, rows, cols] = split(value)

    for first in range(0, quarter, part):
        for j in range(width // LANES):
            cols = slice(j * LANES, (j + 1) * LANES)
            rows = slice(first, first + part)
            x = [x_ref[n * quarter + first : n * quarter + first + part, cols] for n in range(4)]
            keep(odd_ref, rows, cols, x[0] - x[2])
            keep(odd_ref, slice(quarter + first, quarter + first + part), cols, x[1] - x[3])
            left, right = x[0] + x[2], x[1] + x[3]
            keep(two_ref, rows, cols, left - right)
            keep(four_ref, rows, cols, left + right)

    dot = functools.partial(jnp.dot, preferred_element_type=F32)

    def product(high, low, values):
        return dot(high, values[0]) + dot(high, values[1]) + dot(low, values[0])

    def store(start, both):
        count = both.shape[0] // 2
        low = low_half((count, LANES))
        for j in range(CHUNK // 2):
            cols = slice(j * LANES, (j + 1) * LANES)
            real, imag = both[:count, cols], both[count:, cols]
            first = jnp.where(low, real, pltpu.roll(imag, HALF, 1))
            second = jnp.where(low, pltpu.roll(real, HALF, 1), imag)
            for b, value in ((j, first), (j + CHUNK // 2, second)):
                out_ref[pl.ds(start * CHUNK + b, count, stride=CHUNK), :] = value

    for n in range(2):
        rows = slice(2 * n * part, 2 * (n + 1) * part)
        store(2 * n * part, product(odd_high[rows, :], odd_low[rows, :], odd_ref))
    store(part, product(two_high[...], two_low[...], two_ref))
    store(3 * part, product(four_high[...], four_low[...], four_ref))


def transform_scratch(total, width):
    return [
        pltpu.VMEM((total, width), F32),
        pltpu.VMEM((2, total // 2, width), BF16),
        pltpu.VMEM((2, total // 4, width), BF16),
        pltpu.VMEM((2, total // 4, width), BF16),
    ]


def transform_kernel(*refs):
    tables, piece_refs, (out_ref, x_ref, *folded) = refs[:6], refs[6:-5], refs[-5:]
    me = lax.axis_index("tm")
    for m, piece_ref in enumerate(piece_refs):
        times = piece_ref.shape[0]
        rows = pl.ds(pl.multiple_of((me ^ m) * times, times), times)
        x_ref[rows, :] = piece_ref[...]
    transform_columns(tables, x_ref, *folded, out_ref)


def transform(pieces, tables, slots):
    chunks, times, width = pieces[0].shape
    total = times * len(pieces)
    return pl.pallas_call(
        transform_kernel,
        grid=(chunks,),
        in_specs=[pl.BlockSpec(table.shape, lambda n: (0, 0)) for table in tables]
        + [pl.BlockSpec((None, times, width), lambda n: (n, 0, 0))] * len(pieces),
        out_specs=pl.BlockSpec((None, slots * CHUNK, LANES), lambda n: (n, 0, 0)),
        out_shape=pltpu.HBM((chunks, slots * CHUNK, LANES), F32),
        scratch_shapes=transform_scratch(total, width),
        compiler_params=params(40),
        name="transform",
    )(*tables, *in_hbm(pieces))


def first_lane(chunk, chunks):
    return sum(16 * i + 8 for i in range(chunk + 1, chunks))


GROUP = 8


def chunk_tiles(chunk, chunks, weight, parts, before):
    flipped = jnp.where(low_half(weight.shape), weight, -weight)
    width = CHUNK * (chunk + 1)
    stride = width if LANES % width == 0 else 32
    left, right = [], []
    for row in parts:
        row = row[: chunk + 1]
        right.extend((row + row[-1:])[: stride // CHUNK])
        left.append(row[-1] * weight)
        left.append(pltpu.roll(row[-1], HALF, 1) * flipped)
    lh, ll = split(jnp.concatenate(left, axis=0))
    rh, rl = split(jnp.concatenate(right, axis=0))
    full = lax.dot_general(
        jnp.concatenate([lh, ll, lh], axis=1),
        jnp.concatenate([rh, rh, rl], axis=1),
        (((1,), (1,)), ((), ())),
        preferred_element_type=F32,
    )
    if full.shape[1] < LANES:
        full = jnp.concatenate([full] * (LANES // full.shape[1]), axis=1)
    start = first_lane(chunk, chunks)
    row = lax.broadcasted_iota(jnp.int32, (CHUNK, LANES), 0)
    own = lax.broadcasted_iota(jnp.int32, (CHUNK, LANES), 1) - start
    past = own >= width
    corner = (own >= width - CHUNK) & (own < width) & (own - (width - CHUNK) > row)
    valid = (own >= 0) & (own < width + CHUNK * chunk)
    tiles = []
    for k in range(GROUP):
        first = k * stride // LANES * LANES
        real = full[16 * k : 16 * k + 8, first : first + LANES]
        imag = full[16 * k + 8 : 16 * k + 16, first : first + LANES]
        shift = (start - (k * stride - first)) % LANES
        out = pltpu.roll(real, shift, 1)
        out = jnp.where(corner, pltpu.roll(imag, shift, 1), out)
        out = jnp.where(past, pltpu.roll(imag, (shift + width) % LANES, 1), out)
        tiles.append(jnp.where(valid, out, before[k]))
    return tiles


def early_gram_kernel(tile, chunks, scale, z_ref, w_ref, out_ref):
    weight = w_ref[...] * scale

    def step(g, carry):
        parts = []
        for k in range(GROUP):
            rows = pl.ds(pl.multiple_of((g * GROUP + k) * CHUNK, CHUNK), CHUNK)
            parts.append([z_ref[n, rows, :] for n in range(chunks - 1)])
        tiles = [jnp.zeros((CHUNK, LANES), F32)] * GROUP
        for chunk in range(chunks - 1):
            tiles = chunk_tiles(chunk, chunks, weight, parts, tiles)
        for k in range(GROUP):
            out_ref[g * GROUP + k] = tiles[k]
        return carry

    lax.fori_loop(0, tile // GROUP, step, 0, unroll=True)


def early_gram(spectra, weights, slots, tile, total_points):
    chunks = spectra.shape[0] + 1
    return pl.pallas_call(
        functools.partial(early_gram_kernel, tile, chunks, 1.0 / total_points),
        grid=(slots // tile,),
        in_specs=[
            pl.BlockSpec((chunks - 1, tile * CHUNK, LANES), lambda i: (0, i, 0)),
            pl.BlockSpec((1, LANES), lambda i: (0, 0)),
        ],
        out_specs=pl.BlockSpec((tile, 8, LANES), lambda i: (i, 0, 0)),
        out_shape=pltpu.HBM((slots, 8, LANES), F32),
        compiler_params=params(24),
        name="early_gram",
    )(*in_hbm([spectra]), weights)


def copy_tile(source, buffer, sem, base, size, t):
    there = pl.ds(pl.multiple_of(base + t * size, 8), size)
    here = pl.ds(pl.multiple_of(t * size, 8), size)
    if len(source.shape) == 3 and size % CHUNK == 0 and source.shape[1] != CHUNK:
        return pltpu.make_async_copy(source.at[:, there], buffer.at[:, here], sem)
    return pltpu.make_async_copy(source.at[there], buffer.at[here], sem)


def half_base(half, count):
    return pl.multiple_of((lax.axis_index("space") % 2 ^ half) * count, GROUP)


def late_tiles(tile, weight, early_ref, late_at, before_ref, out_ref, wait):
    chunks = early_ref.shape[0] + 1

    def step(g, carry):
        parts, before = [], []
        for k in range(GROUP):
            start = pl.multiple_of((g * GROUP + k) * CHUNK, CHUNK)
            parts.append([early_ref[n, pl.ds(start, CHUNK), :] for n in range(chunks - 1)])
            parts[-1].append(late_at(start))
            before.append(before_ref[g * GROUP + k])
        tiles = chunk_tiles(chunks - 1, chunks, weight, parts, before)
        for k in range(GROUP):
            out_ref[g * GROUP + k] = tiles[k]
        return carry

    groups = tile // GROUP

    def one_tile(t, carry):
        wait(t)
        return lax.fori_loop(0, groups, lambda g, c: step(t * groups + g, c), carry, unroll=True)

    lax.fori_loop(0, out_ref.shape[0] // tile, one_tile, 0)


def late_first_kernel(tile, scale, *refs):
    tables, w_ref, early, before = refs[:6], refs[6], refs[7], refs[8]
    late_ref, out_ref = refs[-12:-10]
    piece_refs = refs[9:-12]
    x_ref, odd_ref, two_ref, four_ref, z_ref, early_ref, before_ref = refs[-10:-3]
    piece_sems, tile_sems, late_sem = refs[-3:]
    count = out_ref.shape[0]
    base = half_base(1, count)
    me = lax.axis_index("tm")
    arrivals = []
    for m, piece_ref in enumerate(piece_refs):
        times = piece_ref.shape[1]
        rows = pl.ds(pl.multiple_of((me ^ m) * times, times), times)
        arrivals.append(pltpu.make_async_copy(piece_ref.at[0], x_ref.at[rows], piece_sems.at[m]))
        arrivals[-1].start()

    def copies(t):
        first = copy_tile(early, early_ref, tile_sems.at[0, t], base * CHUNK, tile * CHUNK, t)
        return first, copy_tile(before, before_ref, tile_sems.at[1, t], base, tile, t)

    for t in range(count // tile):
        for copy in copies(t):
            copy.start()
    for copy in arrivals:
        copy.wait()
    transform_columns(tables, x_ref, odd_ref, two_ref, four_ref, z_ref)
    keep = pltpu.make_async_copy(z_ref, late_ref.at[0], late_sem)
    keep.start()

    def wait(t):
        for copy in copies(t):
            copy.wait()

    late_at = lambda start: z_ref[pl.ds(pl.multiple_of(base * CHUNK + start, 8), CHUNK), :]
    late_tiles(tile, w_ref[...] * scale, early_ref, late_at, before_ref, out_ref, wait)
    keep.wait()


def late_first(pieces, tables, early, weights, before, slots, tile, total_points):
    _, times, width = pieces[0].shape
    total, count = times * len(pieces), slots // 2
    return pl.pallas_call(
        functools.partial(late_first_kernel, tile, 1.0 / total_points),
        in_specs=[pl.BlockSpec(memory_space=pltpu.VMEM)] * (len(tables) + 1)
        + [pl.BlockSpec(memory_space=pl.ANY)] * (2 + len(pieces)),
        out_specs=[
            pl.BlockSpec(memory_space=pl.ANY),
            pl.BlockSpec(memory_space=pltpu.VMEM),
        ],
        out_shape=[
            pltpu.HBM((1, slots * CHUNK, LANES), F32),
            pltpu.HBM((count, CHUNK, LANES), F32),
        ],
        scratch_shapes=transform_scratch(total, width)
        + [
            pltpu.VMEM((slots * CHUNK, LANES), F32),
            pltpu.VMEM((early.shape[0], count * CHUNK, LANES), F32),
            pltpu.VMEM((count, CHUNK, LANES), F32),
            pltpu.SemaphoreType.DMA((len(pieces),)),
            pltpu.SemaphoreType.DMA((2, count // tile)),
            pltpu.SemaphoreType.DMA(()),
        ],
        compiler_params=params(40),
        name="late_first",
    )(*tables, weights, *in_hbm([early, before, *pieces]))


def late_second_kernel(tile, scale, *refs):
    sources, w_ref, out_ref = refs[:3], refs[3], refs[4]
    buffers, sems = refs[5:8], refs[8]
    count = out_ref.shape[0]
    base = half_base(0, count)
    sizes = (tile * CHUNK, tile * CHUNK, tile)

    def copies(t):
        bases = (base * CHUNK, base * CHUNK, base)
        return [
            copy_tile(sources[n], buffers[n], sems.at[n, t], bases[n], sizes[n], t)
            for n in range(3)
        ]

    for t in range(count // tile):
        for copy in copies(t):
            copy.start()

    def wait(t):
        for copy in copies(t):
            copy.wait()

    late_at = lambda start: buffers[1][0, pl.ds(start, CHUNK), :]
    late_tiles(tile, w_ref[...] * scale, buffers[0], late_at, buffers[2], out_ref, wait)


def late_second(early, late, weights, before, slots, tile, total_points):
    count = slots // 2
    sizes = [(z.shape[0], count * CHUNK, LANES) for z in (early, late)]
    sizes.append((count, CHUNK, LANES))
    return pl.pallas_call(
        functools.partial(late_second_kernel, tile, 1.0 / total_points),
        in_specs=[pl.BlockSpec(memory_space=pl.ANY)] * 3
        + [pl.BlockSpec(memory_space=pltpu.VMEM)],
        out_shape=pltpu.HBM((count, CHUNK, LANES), F32),
        scratch_shapes=[pltpu.VMEM(size, F32) for size in sizes]
        + [pltpu.SemaphoreType.DMA((3, count // tile))],
        compiler_params=params(24),
        name="late_second",
    )(*in_hbm([early, late, before]), weights)


def power_kernel(blocks, x_ref, out_ref):
    count = x_ref.shape[2]
    chunks = blocks // CHUNK
    real = [[None] * chunks for _ in range(chunks)]
    imag = [[None] * chunks for _ in range(chunks)]
    for c in range(chunks):
        start = first_lane(c, chunks)
        for d in range(c):
            x = x_ref[start + CHUNK * d : start + CHUNK * (d + 1)]
            y = x_ref[start + CHUNK * (c + 1 + d) : start + CHUNK * (c + 2 + d)]
            real[d][c], real[c][d] = x, jnp.swapaxes(x, 0, 1)
            imag[d][c], imag[c][d] = y, -jnp.swapaxes(y, 0, 1)
        x = x_ref[start + CHUNK * c : start + CHUNK * (c + 1)]
        flip = jnp.swapaxes(x, 0, 1)
        b = lax.broadcasted_iota(jnp.int32, x.shape, 0)
        s = lax.broadcasted_iota(jnp.int32, x.shape, 1)
        real[c][c] = jnp.where(b <= s, x, flip)
        imag[c][c] = jnp.where(b > s, x, jnp.where(b < s, -flip, 0.0))
    whole = lambda m: jnp.concatenate([jnp.concatenate(r, axis=1) for r in m], axis=0)
    real, imag = whole(real), -whole(imag)

    def apply(vr, vi):
        vr, vi = vr[:, None, :], vi[:, None, :]
        return jnp.sum(real * vr - imag * vi, axis=0), jnp.sum(real * vi + imag * vr, axis=0)

    vr = jnp.full((blocks, count), 1.0 / math.sqrt(blocks), F32)
    vi = jnp.zeros((blocks, count), F32)
    for _ in range(POWER):
        ur, ui = apply(vr, vi)
        length = lax.rsqrt(jnp.sum(ur * ur + ui * ui, axis=0, keepdims=True) + 1e-06)
        vr, vi = ur * length, ui * length
    ur, ui = apply(vr, vi)
    energy = jnp.sum(vr * ur + vi * ui, axis=0, keepdims=True)
    out_ref[0:blocks, :] = vr
    out_ref[blocks : 2 * blocks, :] = vi
    out_ref[2 * blocks : 2 * blocks + 8, :] = jnp.broadcast_to(energy, (8, count))


def power(packed, blocks):
    return pl.pallas_call(
        functools.partial(power_kernel, blocks),
        out_shape=jax.ShapeDtypeStruct((2 * blocks + 8, packed.shape[2]), F32),
        compiler_params=params(32),
        name="power",
    )(packed)


def reverse_rows(value):
    row = lax.broadcasted_iota(jnp.int32, (8, LANES), 0)
    tiles = []
    for start in range(0, value.shape[0], 8):
        tile = value[start : start + 8]
        for span in (1, 2, 4):
            upper = (row & span) == 0
            tile = jnp.where(upper, pltpu.roll(tile, 8 - span, 0), pltpu.roll(tile, span, 0))
        tiles.append(tile)
    return jnp.concatenate(tiles[::-1], axis=0)


def modes_kernel(tile, classes, total_times, *refs):
    early, late, v_ref, out_ref, energy_ref, z_ref, s_ref, e_ref, sems = refs
    chunks = z_ref.shape[0]
    blocks = CHUNK * z_ref.shape[0]
    group = 8
    lane = lax.broadcasted_iota(jnp.int32, (group, LANES), 1)
    row = lax.broadcasted_iota(jnp.int32, (group, LANES), 0)
    per_tile = LANES // blocks
    low = low_half((group, LANES))

    def spread(vector):
        vector = jnp.where(lane < blocks, vector, 0.0)
        span = blocks
        while span < LANES:
            vector = vector + pltpu.roll(vector, span, 1)
            span *= 2
        parts = []
        for first in range(0, group, per_tile):
            parts.append(jnp.where(lane // blocks + first == row, vector, 0.0))
        return jnp.concatenate(parts, axis=1)

    def step(g, carry):
        start = pl.multiple_of(g * group, group)
        vec = v_ref[pl.ds(start, group), :]
        both = jnp.concatenate([spread(vec), spread(pltpu.roll(vec, LANES - blocks, 1))], axis=0)
        vh, vl = split(both)
        z = []
        for k in range(group):
            rows = pl.ds(pl.multiple_of((g * group + k) * CHUNK, CHUNK), CHUNK)
            z.append(z_ref[:, rows, :].reshape(blocks, LANES))
        zh, zl = split(jnp.concatenate(z, axis=0))
        full = jnp.dot(
            jnp.concatenate([vh, vl], axis=0),
            jnp.concatenate([zh, zl], axis=1),
            preferred_element_type=F32,
        )
        sums = full[:16, :LANES] + full[:16, LANES:] + full[16:, :LANES]
        turned = pltpu.roll(sums[8:], HALF, 1)
        value = sums[:8] + jnp.where(low, -turned, turned)
        energy = jnp.broadcast_to(vec[:, 2 * blocks : 2 * blocks + 1], (group, LANES))
        s_ref[pl.ds(start, group), :] = value * lax.rsqrt(energy + 1e-06)
        e_ref[pl.ds(start, group), :] = energy
        return carry

    groups = tile // group
    tiles = v_ref.shape[0] // tile

    def copies(t):
        rows = pl.ds(pl.multiple_of(t * tile * CHUNK, CHUNK), tile * CHUNK)
        first, second = z_ref.at[: chunks - 1, rows], z_ref.at[chunks - 1 :, rows]
        return (
            pltpu.make_async_copy(early.at[:, rows], first, sems.at[0, t]),
            pltpu.make_async_copy(late.at[:, rows], second, sems.at[1, t]),
        )

    for t in range(tiles):
        for copy in copies(t):
            copy.start()

    def one_tile(t, carry):
        for copy in copies(t):
            copy.wait()
        return lax.fori_loop(0, groups, lambda g, c: step(t * groups + g, c), carry, unroll=True)

    lax.fori_loop(0, tiles, one_tile, 0)

    half = out_ref.shape[0] // classes // 2
    bits = classes.bit_length() - 1
    low = low_half((half, LANES))
    for d in range(classes):
        r = bit_reverse(d, bits)
        direct = pl.ds(slot_of(r, total_times), half, stride=classes // 4)
        mirror = pl.ds(slot_of(classes - r, total_times), half, stride=classes // 4)
        start = 2 * half * d
        out_ref[start : start + half, :] = s_ref[direct, :]
        energy_ref[start : start + half, :] = e_ref[direct, :]
        turned = reverse_rows(s_ref[mirror, :])
        out_ref[start + half : start + 2 * half, :] = jnp.where(low, turned, -turned)
        energy_ref[start + half : start + 2 * half, :] = reverse_rows(e_ref[mirror, :])


def modes(early, late, vectors, total, classes, slots, tile):
    return pl.pallas_call(
        functools.partial(modes_kernel, tile, classes, total),
        in_specs=[
            pl.BlockSpec(memory_space=pl.ANY),
            pl.BlockSpec(memory_space=pl.ANY),
            pl.BlockSpec(memory_space=pltpu.VMEM),
        ],
        out_shape=[jax.ShapeDtypeStruct((total, LANES), F32)] * 2,
        scratch_shapes=[
            pltpu.VMEM((early.shape[0] + 1, *early.shape[1:]), F32),
            pltpu.VMEM((slots, LANES), F32),
            pltpu.VMEM((slots, LANES), F32),
            pltpu.SemaphoreType.DMA((2, slots // tile)),
        ],
        compiler_params=params(24),
        name="modes",
    )(*in_hbm([early, late]), vectors)


def place_kernel(x_ref, out_ref):
    low = low_half(x_ref.shape[1:])
    for i in range(x_ref.shape[0] // 2):
        first, second = x_ref[2 * i], x_ref[2 * i + 1]
        cols = slice(i * LANES, (i + 1) * LANES)
        out_ref[0, :, cols] = jnp.where(low, first, pltpu.roll(second, HALF, 1))
        out_ref[1, :, cols] = jnp.where(low, pltpu.roll(first, HALF, 1), second)


def place(pieces):
    count, rows, _ = pieces.shape
    return pl.pallas_call(
        place_kernel,
        out_shape=jax.ShapeDtypeStruct((2, rows, count * HALF), F32),
        compiler_params=params(32),
        name="place",
    )(pieces)


def exchange(value, axes):
    return lax.all_to_all(value, axes, 0, 0, tiled=True)


def body(mesh_shape, snapshots, quad_weights):
    tm_size, space_size = mesh_shape["tm"], mesh_shape["space"]
    local_times, blocks, points = snapshots.shape
    total_times = local_times * tm_size
    total_points = points * space_size
    devices = tm_size * space_size
    per_device = -(-(total_times // 2 + 1) // devices)
    slots = per_device * devices
    tile = slots // 4
    tables = transform_tables(total_times, slots)
    window = jnp.asarray(window_table(total_times))

    here = lax.axis_index("tm") * HALF
    weights = lax.dynamic_slice(quad_weights, (here,), (HALF,))
    weights = jnp.concatenate([weights, weights])[None, :]

    chunks = blocks // CHUNK

    def send(group, offsets, after):
        sent = dict(zip(offsets, pack(snapshots, window, group, tuple(offsets), after)))
        flying = {}
        for m, part in sent.items():
            pairs = [(d, d ^ m) for d in range(tm_size)]
            flying[m] = lax.ppermute(part, "tm", pairs) if m else part
        return sent, flying

    half, quarter = tm_size // 2, tm_size // 4
    first = [*range(half, half + quarter), *range(quarter)]
    second = [*range(half + quarter, tm_size), *range(quarter, half)]
    group = range(chunks - 1)
    sent, pieces = send(group, first[:1], [])
    sent, more = send(group, first[1:], [sent[half]])
    pieces |= more
    pieces |= send(group, second, [sent[0]])[1]
    group = range(chunks - 1, chunks)
    sent, last = send(group, first, [pieces[half]])
    last |= send(group, second, [sent[0], pieces[half + quarter]])[1]
    ordered = lambda pieces: [pieces[m] for m in range(tm_size)]
    early = transform(ordered(pieces), tables, slots)
    matrices = early_gram(early, weights, slots, tile, total_points)
    late, given = late_first(
        ordered(last), tables, early, weights, matrices, slots, tile, total_points
    )

    space = lax.axis_index("space")

    def swap(value, level):
        pairs = [(i, i ^ (1 << level)) for i in range(space_size)]
        return lax.ppermute(value, "space", pairs)

    arriving = swap(given, 0)
    part = late_second(early, late, weights, matrices, slots, tile, total_points)
    levels = space_size.bit_length() - 1
    shape = (*[2] * (levels - 1), tm_size, per_device, *part.shape[1:])
    part, arriving = part.reshape(shape), arriving.reshape(shape)
    bit = space // 2
    pick = lambda value, i: lax.dynamic_index_in_dim(value, i, 0, keepdims=False)
    cut = 2 * per_device // 3
    given = pick(part, 1 - bit)[:, :cut] + pick(arriving, 1 - bit)[:, :cut]
    kept = pick(part, bit)[:, :cut] + pick(arriving, bit)[:, :cut]
    given = swap(given, 1)
    rest = part[:, :, cut:] + arriving[:, :, cut:]
    rest = lax.all_to_all(rest, "tm", 1, 1, tiled=True).sum(axis=1)
    rest = pick(rest, bit) + swap(pick(rest, 1 - bit), 1)
    part = exchange(kept + given, "tm").sum(axis=0)
    part = jnp.concatenate([part, rest], axis=0)

    vectors = power(part.transpose(2, 1, 0), blocks).T
    vectors = jnp.pad(vectors, ((0, 0), (0, LANES - vectors.shape[1])))
    vectors = jnp.broadcast_to(vectors[None], (devices, per_device, LANES))
    vectors = exchange(vectors, ("tm", "space"))
    vectors = vectors.reshape(tm_size, *[2] * levels, per_device, LANES)
    vectors = vectors.transpose(*range(levels, -1, -1), levels + 1, levels + 2)
    vectors = vectors.reshape(slots, LANES)

    pieces, energies = modes(early, late, vectors, total_times, tm_size, slots, tile)
    pieces = exchange(pieces.reshape(tm_size, local_times, LANES), "tm")
    energies = energies.reshape(tm_size, local_times, LANES)[:, :, 0]
    energies = lax.dynamic_index_in_dim(energies, lax.axis_index("tm"), 0, keepdims=False)
    return place(pieces), energies


def fits(mesh_shape, times, blocks, points):
    tm_size, space_size = mesh_shape["tm"], mesh_shape["space"]
    return (
        points == space_size * tm_size * HALF
        and (tm_size, space_size) == (8, 4)
        and space_size & (space_size - 1) == 0
        and times % (tm_size * 8) == 0
        and blocks % CHUNK == 0
        and blocks == 32
    )


def matvec(matrix, vector):
    return jnp.einsum("fbc,fc->fb", matrix, vector, precision=lax.Precision.HIGHEST)


def power_modes(real_gram, imag_gram):
    vec_real = jnp.ones(real_gram.shape[:2], jnp.float32) / math.sqrt(real_gram.shape[1])
    vec_imag = jnp.zeros(real_gram.shape[:2], jnp.float32)
    for sweep_idx in range(POWER):
        new_real = matvec(real_gram, vec_real) - matvec(imag_gram, vec_imag)
        new_imag = matvec(real_gram, vec_imag) + matvec(imag_gram, vec_real)
        length = lax.rsqrt(
            jnp.sum(new_real * new_real + new_imag * new_imag, axis=1, keepdims=True) + 1e-06
        )
        vec_real = new_real * length
        vec_imag = new_imag * length
    image_real = matvec(real_gram, vec_real) - matvec(imag_gram, vec_imag)
    image_imag = matvec(real_gram, vec_imag) + matvec(imag_gram, vec_real)
    energy = jnp.sum(vec_real * image_real + vec_imag * image_imag, axis=1)
    return (vec_real, vec_imag, energy)


def general_body(snapshots, quad_weights):
    tm_size = lax.axis_size("tm")
    bit_count = tm_size.bit_length() - 1
    local_times, blocks, points = snapshots.shape
    total_times = local_times * tm_size
    total_points = points * lax.axis_size("space")
    norm_factor = 1.0 / math.sqrt(0.375 * total_times)
    flattened = snapshots.reshape(local_times, blocks * points)
    columns = lax.all_to_all(flattened, "tm", split_axis=1, concat_axis=0, tiled=True)
    col_count = columns.shape[1]
    times_all = jnp.arange(total_times, dtype=jnp.int32)
    window = (
        0.5 - 0.5 * jnp.cos(2.0 * math.pi * times_all.astype(jnp.float32) / total_times)
    ) * norm_factor
    row_block = min(256, total_times)

    def one_block(block_idx):
        row_ids = block_idx * row_block + jnp.arange(row_block, dtype=jnp.int32)
        frequency = bit_reverse(row_ids // local_times, bit_count) + tm_size * (
            row_ids % local_times
        )
        angles = (
            -2.0
            * math.pi
            * (frequency[:, None] * times_all[None, :] % total_times).astype(jnp.float32)
            / total_times
        )
        cos_tab = jnp.cos(angles) * window[None, :]
        sin_tab = jnp.sin(angles) * window[None, :]
        return (
            jnp.dot(cos_tab, columns, precision=lax.Precision.HIGHEST),
            jnp.dot(sin_tab, columns, precision=lax.Precision.HIGHEST),
        )

    spec_real, spec_imag = lax.map(one_block, jnp.arange(total_times // row_block, dtype=jnp.int32))
    spectrum = jnp.stack(
        [spec_real.reshape(total_times, col_count), spec_imag.reshape(total_times, col_count)]
    )
    returned = lax.all_to_all(spectrum, "tm", split_axis=1, concat_axis=2, tiled=True)
    spectral = returned.reshape(2, local_times, blocks, points)
    weighted = spectral * quad_weights
    gram_full = (
        jnp.einsum("pfbx,qfcx->fpbqc", weighted, spectral, precision=lax.Precision.HIGHEST)
        / total_points
    )
    real_gram = gram_full[:, 0, :, 0] + gram_full[:, 1, :, 1]
    imag_gram = gram_full[:, 0, :, 1] - gram_full[:, 1, :, 0]
    real_gram, imag_gram = lax.psum((real_gram, imag_gram), "space")
    vec_real, vec_imag, energy = power_modes(real_gram, imag_gram)
    inverse_root = lax.rsqrt(energy + 1e-06)[:, None]
    modes_real = jnp.einsum(
        "fb,fbx->fx", vec_real, spectral[0], precision=lax.Precision.HIGHEST
    ) - jnp.einsum("fb,fbx->fx", vec_imag, spectral[1], precision=lax.Precision.HIGHEST)
    modes_imag = jnp.einsum(
        "fb,fbx->fx", vec_imag, spectral[0], precision=lax.Precision.HIGHEST
    ) + jnp.einsum("fb,fbx->fx", vec_real, spectral[1], precision=lax.Precision.HIGHEST)
    return (jnp.stack([modes_real * inverse_root, modes_imag * inverse_root]), energy)


def solution(mesh):
    shape = dict(mesh.shape)

    def program(snapshots, quad_weights):
        chosen = general_body
        if fits(shape, *snapshots.shape):
            chosen = functools.partial(body, shape)
        return jax.shard_map(
            chosen,
            mesh=mesh,
            in_specs=(P("tm", None, "space"), P("space")),
            out_specs=(P(None, "tm", "space"), P("tm")),
            check_vma=False,
        )(snapshots, quad_weights)

    return program
```

```python
import functools
import math

import jax
import jax.numpy as jnp
import ml_dtypes
import numpy as np
from jax import lax
from jax.experimental import pallas as pl
from jax.experimental.pallas import tpu as pltpu
from jax.sharding import PartitionSpec as P

POWER = 3
CHUNK = 8
HALF = 64
LANES = 128
BF16 = jnp.bfloat16
F32 = jnp.float32


def bit_reverse(value, bit_count):
    return sum((value >> i & 1) << (bit_count - 1 - i) for i in range(bit_count))


def split_np(table):
    high = table.astype(ml_dtypes.bfloat16)
    low = (table - high.astype(np.float64)).astype(ml_dtypes.bfloat16)
    return high, low


def split(value):
    high = value.astype(BF16)
    return high, (value - high.astype(F32)).astype(BF16)


def low_half(shape):
    return lax.broadcasted_iota(jnp.int32, shape, len(shape) - 1) < HALF


def in_hbm(arrays):
    return [pltpu.with_memory_space_constraint(array, pltpu.HBM) for array in arrays]


def params(mib):
    return pltpu.CompilerParams(vmem_limit_bytes=mib * 2**20)


def slot_of(freq, total_times):
    part = total_times // 8
    return (freq - 1) % 4 * part + freq // 4


@functools.lru_cache(None)
def transform_tables(total_times, slots):
    part, quarter = total_times // 8, total_times // 4
    t = np.arange(quarter)

    def waves(rest, count):
        k = 4 * np.arange(count) + rest
        phase = 2 * np.pi * (k[:, None] * t[None, :] % total_times) / total_times
        live = (k <= total_times // 2)[:, None]
        return np.cos(phase) * live, np.sin(phase) * live

    c, s = waves(1, part)
    ones = np.block([[c, -s], [-s, -c]])
    c, s = waves(3, part)
    threes = np.block([[c, s], [-s, c]])
    c, s = waves(2, part)
    twos = np.concatenate([c, -s])
    c, s = waves(0, slots - 3 * part)
    fours = np.concatenate([c, -s])
    odd = split_np(np.concatenate([ones, threes]))
    return (*odd, *split_np(twos), *split_np(fours))


@functools.lru_cache(None)
def window_table(total_times):
    t = np.arange(total_times)
    window = (0.5 - 0.5 * np.cos(2 * np.pi * t / total_times)) / math.sqrt(0.375 * total_times)
    return np.broadcast_to(window[:, None], (total_times, LANES)).astype(np.float32)


def pack_kernel(offsets, *refs):
    x_refs, out_refs = refs[: len(offsets)], refs[-len(offsets) :]
    window = refs[len(offsets)][...]
    times = window.shape[0]
    low = low_half((times, LANES))
    me = lax.axis_index("tm")
    for m, x_ref, out_ref in zip(offsets, x_refs, out_refs):
        blocks = x_ref.shape[1]
        rows = x_ref.reshape(times * blocks, LANES)
        even = (m ^ me) % 2 == 0
        for n in range(out_ref.shape[0]):
            for j in range(CHUNK // 2):
                b = n * CHUNK + j
                first = rows[pl.ds(b, times, stride=blocks), :] * window
                second = rows[pl.ds(b + CHUNK // 2, times, stride=blocks), :] * window
                left = jnp.where(low, first, pltpu.roll(second, HALF, 1))
                right = jnp.where(low, pltpu.roll(first, HALF, 1), second)
                out_ref[n, :, j * LANES : (j + 1) * LANES] = jnp.where(even, left, right)


def pack(snapshots, window, chunks, offsets, after):
    times = snapshots.shape[0]
    count, width = len(chunks), CHUNK * HALF

    def tile_spec(m):
        place = lambda _: (0, chunks[0] // count, m // 2 ^ lax.axis_index("tm") // 2)
        return pl.BlockSpec((times, CHUNK * count, LANES), place)

    return pl.pallas_call(
        functools.partial(pack_kernel, offsets),
        grid=(1,),
        in_specs=[tile_spec(m) for m in offsets]
        + [pl.BlockSpec((times, LANES), lambda _: (lax.axis_index("tm"), 0))]
        + [pl.BlockSpec(memory_space=pl.ANY)] * len(after),
        out_specs=[pl.BlockSpec((count, times, width), lambda _: (0, 0, 0))] * len(offsets),
        out_shape=[pltpu.HBM((count, times, width), F32)] * len(offsets),
        compiler_params=params(40),
        name="pack",
    )(*in_hbm([snapshots] * len(offsets) + [window, *after]))


def transform_columns(tables, x_ref, odd_ref, two_ref, four_ref, out_ref):
    odd_high, odd_low, two_high, two_low, four_high, four_low = tables
    total, width = x_ref.shape
    quarter, part = total // 4, total // 8

    def keep(ref, rows, cols, value):
        ref[0, rows, cols], ref[1, rows, cols] = split(value)

    for first in range(0, quarter, part):
        for j in range(width // LANES):
            cols = slice(j * LANES, (j + 1) * LANES)
            rows = slice(first, first + part)
            x = [x_ref[n * quarter + first : n * quarter + first + part, cols] for n in range(4)]
            keep(odd_ref, rows, cols, x[0] - x[2])
            keep(odd_ref, slice(quarter + first, quarter + first + part), cols, x[1] - x[3])
            left, right = x[0] + x[2], x[1] + x[3]
            keep(two_ref, rows, cols, left - right)
            keep(four_ref, rows, cols, left + right)

    dot = functools.partial(jnp.dot, preferred_element_type=F32)

    def product(high, low, values):
        return dot(high, values[0]) + dot(high, values[1]) + dot(low, values[0])

    def store(start, both):
        count = both.shape[0] // 2
        low = low_half((count, LANES))
        for j in range(CHUNK // 2):
            cols = slice(j * LANES, (j + 1) * LANES)
            real, imag = both[:count, cols], both[count:, cols]
            first = jnp.where(low, real, pltpu.roll(imag, HALF, 1))
            second = jnp.where(low, pltpu.roll(real, HALF, 1), imag)
            for b, value in ((j, first), (j + CHUNK // 2, second)):
                out_ref[pl.ds(start * CHUNK + b, count, stride=CHUNK), :] = value

    for n in range(2):
        rows = slice(2 * n * part, 2 * (n + 1) * part)
        store(2 * n * part, product(odd_high[rows, :], odd_low[rows, :], odd_ref))
    store(part, product(two_high[...], two_low[...], two_ref))
    store(3 * part, product(four_high[...], four_low[...], four_ref))


def transform_scratch(total, width):
    return [
        pltpu.VMEM((total, width), F32),
        pltpu.VMEM((2, total // 2, width), BF16),
        pltpu.VMEM((2, total // 4, width), BF16),
        pltpu.VMEM((2, total // 4, width), BF16),
    ]


def transform_kernel(*refs):
    tables, piece_refs, (out_ref, x_ref, *folded) = refs[:6], refs[6:-5], refs[-5:]
    me = lax.axis_index("tm")
    for m, piece_ref in enumerate(piece_refs):
        times = piece_ref.shape[0]
        rows = pl.ds(pl.multiple_of((me ^ m) * times, times), times)
        x_ref[rows, :] = piece_ref[...]
    transform_columns(tables, x_ref, *folded, out_ref)


def transform(pieces, tables, slots):
    chunks, times, width = pieces[0].shape
    total = times * len(pieces)
    return pl.pallas_call(
        transform_kernel,
        grid=(chunks,),
        in_specs=[pl.BlockSpec(table.shape, lambda n: (0, 0)) for table in tables]
        + [pl.BlockSpec((None, times, width), lambda n: (n, 0, 0))] * len(pieces),
        out_specs=pl.BlockSpec((None, slots * CHUNK, LANES), lambda n: (n, 0, 0)),
        out_shape=pltpu.HBM((chunks, slots * CHUNK, LANES), F32),
        scratch_shapes=transform_scratch(total, width),
        compiler_params=params(40),
        name="transform",
    )(*tables, *in_hbm(pieces))


def first_lane(chunk, chunks):
    return sum(16 * i + 8 for i in range(chunk + 1, chunks))


GROUP = 8


def chunk_tiles(chunk, chunks, weight, parts, before):
    flipped = jnp.where(low_half(weight.shape), weight, -weight)
    width = CHUNK * (chunk + 1)
    stride = width if LANES % width == 0 else 32
    left, right = [], []
    for row in parts:
        row = row[: chunk + 1]
        right.extend((row + row[-1:])[: stride // CHUNK])
        left.append(row[-1] * weight)
        left.append(pltpu.roll(row[-1], HALF, 1) * flipped)
    lh, ll = split(jnp.concatenate(left, axis=0))
    rh, rl = split(jnp.concatenate(right, axis=0))
    full = lax.dot_general(
        jnp.concatenate([lh, ll, lh], axis=1),
        jnp.concatenate([rh, rh, rl], axis=1),
        (((1,), (1,)), ((), ())),
        preferred_element_type=F32,
    )
    if full.shape[1] < LANES:
        full = jnp.concatenate([full] * (LANES // full.shape[1]), axis=1)
    start = first_lane(chunk, chunks)
    row = lax.broadcasted_iota(jnp.int32, (CHUNK, LANES), 0)
    own = lax.broadcasted_iota(jnp.int32, (CHUNK, LANES), 1) - start
    past = own >= width
    corner = (own >= width - CHUNK) & (own < width) & (own - (width - CHUNK) > row)
    valid = (own >= 0) & (own < width + CHUNK * chunk)
    tiles = []
    for k in range(GROUP):
        first = k * stride // LANES * LANES
        real = full[16 * k : 16 * k + 8, first : first + LANES]
        imag = full[16 * k + 8 : 16 * k + 16, first : first + LANES]
        shift = (start - (k * stride - first)) % LANES
        out = pltpu.roll(real, shift, 1)
        out = jnp.where(corner, pltpu.roll(imag, shift, 1), out)
        out = jnp.where(past, pltpu.roll(imag, (shift + width) % LANES, 1), out)
        tiles.append(jnp.where(valid, out, before[k]))
    return tiles


def early_gram_kernel(tile, chunks, scale, z_ref, w_ref, out_ref):
    weight = w_ref[...] * scale

    def step(g, carry):
        parts = []
        for k in range(GROUP):
            rows = pl.ds(pl.multiple_of((g * GROUP + k) * CHUNK, CHUNK), CHUNK)
            parts.append([z_ref[n, rows, :] for n in range(chunks - 1)])
        tiles = [jnp.zeros((CHUNK, LANES), F32)] * GROUP
        for chunk in range(chunks - 1):
            tiles = chunk_tiles(chunk, chunks, weight, parts, tiles)
        for k in range(GROUP):
            out_ref[g * GROUP + k] = tiles[k]
        return carry

    lax.fori_loop(0, tile // GROUP, step, 0, unroll=True)


def early_gram(spectra, weights, slots, tile, total_points):
    chunks = spectra.shape[0] + 1
    return pl.pallas_call(
        functools.partial(early_gram_kernel, tile, chunks, 1.0 / total_points),
        grid=(slots // tile,),
        in_specs=[
            pl.BlockSpec((chunks - 1, tile * CHUNK, LANES), lambda i: (0, i, 0)),
            pl.BlockSpec((1, LANES), lambda i: (0, 0)),
        ],
        out_specs=pl.BlockSpec((tile, 8, LANES), lambda i: (i, 0, 0)),
        out_shape=pltpu.HBM((slots, 8, LANES), F32),
        compiler_params=params(24),
        name="early_gram",
    )(*in_hbm([spectra]), weights)


def copy_tile(source, buffer, sem, base, size, t):
    there = pl.ds(pl.multiple_of(base + t * size, 8), size)
    here = pl.ds(pl.multiple_of(t * size, 8), size)
    if len(source.shape) == 3 and size % CHUNK == 0 and source.shape[1] != CHUNK:
        return pltpu.make_async_copy(source.at[:, there], buffer.at[:, here], sem)
    return pltpu.make_async_copy(source.at[there], buffer.at[here], sem)


def half_base(half, count):
    return pl.multiple_of((lax.axis_index("space") % 2 ^ half) * count, GROUP)


def late_tiles(tile, weight, early_ref, late_at, before_ref, out_ref, wait):
    chunks = early_ref.shape[0] + 1

    def step(g, carry):
        parts, before = [], []
        for k in range(GROUP):
            start = pl.multiple_of((g * GROUP + k) * CHUNK, CHUNK)
            parts.append([early_ref[n, pl.ds(start, CHUNK), :] for n in range(chunks - 1)])
            parts[-1].append(late_at(start))
            before.append(before_ref[g * GROUP + k])
        tiles = chunk_tiles(chunks - 1, chunks, weight, parts, before)
        for k in range(GROUP):
            out_ref[g * GROUP + k] = tiles[k]
        return carry

    groups = tile // GROUP

    def one_tile(t, carry):
        wait(t)
        return lax.fori_loop(0, groups, lambda g, c: step(t * groups + g, c), carry, unroll=True)

    lax.fori_loop(0, out_ref.shape[0] // tile, one_tile, 0)


def late_first_kernel(tile, scale, *refs):
    tables, w_ref, early, before = refs[:6], refs[6], refs[7], refs[8]
    late_ref, out_ref = refs[-12:-10]
    piece_refs = refs[9:-12]
    x_ref, odd_ref, two_ref, four_ref, z_ref, early_ref, before_ref = refs[-10:-3]
    piece_sems, tile_sems, late_sem = refs[-3:]
    count = out_ref.shape[0]
    base = half_base(1, count)
    me = lax.axis_index("tm")
    arrivals = []
    for m, piece_ref in enumerate(piece_refs):
        times = piece_ref.shape[1]
        rows = pl.ds(pl.multiple_of((me ^ m) * times, times), times)
        arrivals.append(pltpu.make_async_copy(piece_ref.at[0], x_ref.at[rows], piece_sems.at[m]))
        arrivals[-1].start()

    def copies(t):
        first = copy_tile(early, early_ref, tile_sems.at[0, t], base * CHUNK, tile * CHUNK, t)
        return first, copy_tile(before, before_ref, tile_sems.at[1, t], base, tile, t)

    for t in range(count // tile):
        for copy in copies(t):
            copy.start()
    for copy in arrivals:
        copy.wait()
    transform_columns(tables, x_ref, odd_ref, two_ref, four_ref, z_ref)
    keep = pltpu.make_async_copy(z_ref, late_ref.at[0], late_sem)
    keep.start()

    def wait(t):
        for copy in copies(t):
            copy.wait()

    late_at = lambda start: z_ref[pl.ds(pl.multiple_of(base * CHUNK + start, 8), CHUNK), :]
    late_tiles(tile, w_ref[...] * scale, early_ref, late_at, before_ref, out_ref, wait)
    keep.wait()


def late_first(pieces, tables, early, weights, before, slots, tile, total_points):
    _, times, width = pieces[0].shape
    total, count = times * len(pieces), slots // 2
    return pl.pallas_call(
        functools.partial(late_first_kernel, tile, 1.0 / total_points),
        in_specs=[pl.BlockSpec(memory_space=pltpu.VMEM)] * (len(tables) + 1)
        + [pl.BlockSpec(memory_space=pl.ANY)] * (2 + len(pieces)),
        out_specs=[
            pl.BlockSpec(memory_space=pl.ANY),
            pl.BlockSpec(memory_space=pltpu.VMEM),
        ],
        out_shape=[
            pltpu.HBM((1, slots * CHUNK, LANES), F32),
            pltpu.HBM((count, CHUNK, LANES), F32),
        ],
        scratch_shapes=transform_scratch(total, width)
        + [
            pltpu.VMEM((slots * CHUNK, LANES), F32),
            pltpu.VMEM((early.shape[0], count * CHUNK, LANES), F32),
            pltpu.VMEM((count, CHUNK, LANES), F32),
            pltpu.SemaphoreType.DMA((len(pieces),)),
            pltpu.SemaphoreType.DMA((2, count // tile)),
            pltpu.SemaphoreType.DMA(()),
        ],
        compiler_params=params(40),
        name="late_first",
    )(*tables, weights, *in_hbm([early, before, *pieces]))


def late_second_kernel(tile, scale, *refs):
    sources, w_ref, out_ref = refs[:3], refs[3], refs[4]
    buffers, sems = refs[5:8], refs[8]
    count = out_ref.shape[0]
    base = half_base(0, count)
    sizes = (tile * CHUNK, tile * CHUNK, tile)

    def copies(t):
        bases = (base * CHUNK, base * CHUNK, base)
        return [
            copy_tile(sources[n], buffers[n], sems.at[n, t], bases[n], sizes[n], t)
            for n in range(3)
        ]

    for t in range(count // tile):
        for copy in copies(t):
            copy.start()

    def wait(t):
        for copy in copies(t):
            copy.wait()

    late_at = lambda start: buffers[1][0, pl.ds(start, CHUNK), :]
    late_tiles(tile, w_ref[...] * scale, buffers[0], late_at, buffers[2], out_ref, wait)


def late_second(early, late, weights, before, slots, tile, total_points):
    count = slots // 2
    sizes = [(z.shape[0], count * CHUNK, LANES) for z in (early, late)]
    sizes.append((count, CHUNK, LANES))
    return pl.pallas_call(
        functools.partial(late_second_kernel, tile, 1.0 / total_points),
        in_specs=[pl.BlockSpec(memory_space=pl.ANY)] * 3
        + [pl.BlockSpec(memory_space=pltpu.VMEM)],
        out_shape=pltpu.HBM((count, CHUNK, LANES), F32),
        scratch_shapes=[pltpu.VMEM(size, F32) for size in sizes]
        + [pltpu.SemaphoreType.DMA((3, count // tile))],
        compiler_params=params(24),
        name="late_second",
    )(*in_hbm([early, late, before]), weights)


def power_kernel(blocks, x_ref, out_ref):
    count = x_ref.shape[2]
    chunks = blocks // CHUNK
    real = [[None] * chunks for _ in range(chunks)]
    imag = [[None] * chunks for _ in range(chunks)]
    for c in range(chunks):
        start = first_lane(c, chunks)
        for d in range(c):
            x = x_ref[start + CHUNK * d : start + CHUNK * (d + 1)]
            y = x_ref[start + CHUNK * (c + 1 + d) : start + CHUNK * (c + 2 + d)]
            real[d][c], real[c][d] = x, jnp.swapaxes(x, 0, 1)
            imag[d][c], imag[c][d] = y, -jnp.swapaxes(y, 0, 1)
        x = x_ref[start + CHUNK * c : start + CHUNK * (c + 1)]
        flip = jnp.swapaxes(x, 0, 1)
        b = lax.broadcasted_iota(jnp.int32, x.shape, 0)
        s = lax.broadcasted_iota(jnp.int32, x.shape, 1)
        real[c][c] = jnp.where(b <= s, x, flip)
        imag[c][c] = jnp.where(b > s, x, jnp.where(b < s, -flip, 0.0))
    whole = lambda m: jnp.concatenate([jnp.concatenate(r, axis=1) for r in m], axis=0)
    real, imag = whole(real), -whole(imag)

    def apply(vr, vi):
        vr, vi = vr[:, None, :], vi[:, None, :]
        return jnp.sum(real * vr - imag * vi, axis=0), jnp.sum(real * vi + imag * vr, axis=0)

    vr = jnp.full((blocks, count), 1.0 / math.sqrt(blocks), F32)
    vi = jnp.zeros((blocks, count), F32)
    for _ in range(POWER):
        ur, ui = apply(vr, vi)
        length = lax.rsqrt(jnp.sum(ur * ur + ui * ui, axis=0, keepdims=True) + 1e-06)
        vr, vi = ur * length, ui * length
    ur, ui = apply(vr, vi)
    energy = jnp.sum(vr * ur + vi * ui, axis=0, keepdims=True)
    columns = jnp.concatenate([vr, vi, jnp.broadcast_to(energy, (8, count))], axis=0)
    columns = jnp.pad(columns, ((0, LANES - columns.shape[0]), (0, LANES - count)))
    rows = columns.T
    half = count // 2
    low = low_half((half, LANES))
    lane = lax.broadcasted_iota(jnp.int32, (half, LANES), 1)
    first, second = rows[:half], rows[half : 2 * half]
    last = jnp.broadcast_to(rows[2 * half : count], (half, LANES))
    ends = jnp.where(lane == 2, pltpu.roll(last, HALF + 2, 1), pltpu.roll(last, HALF, 1))
    ends = jnp.where(lane == 1, pltpu.roll(second, HALF + 1, 1), ends)
    out_ref[half:] = jnp.where(lane == 0, pltpu.roll(first, HALF, 1), ends)
    out_ref[:half] = jnp.where(low, first, pltpu.roll(second, HALF, 1))


def power(packed, blocks):
    return pl.pallas_call(
        functools.partial(power_kernel, blocks),
        out_shape=jax.ShapeDtypeStruct((packed.shape[2] // 2 * 2, LANES), F32),
        compiler_params=params(32),
        name="power",
    )(packed)


def reverse_rows(value):
    row = lax.broadcasted_iota(jnp.int32, (8, LANES), 0)
    tiles = []
    for start in range(0, value.shape[0], 8):
        tile = value[start : start + 8]
        for span in (1, 2, 4):
            upper = (row & span) == 0
            tile = jnp.where(upper, pltpu.roll(tile, 8 - span, 0), pltpu.roll(tile, span, 0))
        tiles.append(tile)
    return jnp.concatenate(tiles[::-1], axis=0)


def unpack_vectors(packed_ref, v_ref, classes):
    devices, rows, _ = packed_ref.shape
    half = rows // 2
    count = v_ref.shape[0] // devices
    spaces = devices // classes
    low = low_half((half, LANES))
    for device in range(devices):
        tau, space = divmod(device, spaces)
        order = bit_reverse(space, spaces.bit_length() - 1)
        start = (order * classes + tau) * count
        vector, ends = packed_ref[device, :half, :], packed_ref[device, half:, :]
        turned = pltpu.roll(ends, HALF, 1)
        v_ref[start : start + half, :] = jnp.where(low, vector, turned)
        second = jnp.where(low, pltpu.roll(vector, HALF, 1), pltpu.roll(ends, HALF - 1, 1))
        v_ref[start + half : start + 2 * half, :] = second
        last = jnp.where(low, turned, pltpu.roll(ends, HALF - 2, 1))
        v_ref[start + 2 * half : start + count, :] = last[:1]


def modes_kernel(tile, classes, total_times, *refs):
    early, late, packed_ref, out_ref, energy_ref, z_ref, s_ref, e_ref, v_ref, sems = refs
    chunks = z_ref.shape[0]
    blocks = CHUNK * z_ref.shape[0]
    group = 8
    lane = lax.broadcasted_iota(jnp.int32, (group, LANES), 1)
    row = lax.broadcasted_iota(jnp.int32, (group, LANES), 0)
    per_tile = LANES // blocks
    low = low_half((group, LANES))

    def spread(vector):
        vector = jnp.where(lane < blocks, vector, 0.0)
        span = blocks
        while span < LANES:
            vector = vector + pltpu.roll(vector, span, 1)
            span *= 2
        parts = []
        for first in range(0, group, per_tile):
            parts.append(jnp.where(lane // blocks + first == row, vector, 0.0))
        return jnp.concatenate(parts, axis=1)

    def step(g, carry):
        start = pl.multiple_of(g * group, group)
        vec = v_ref[pl.ds(start, group), :]
        both = jnp.concatenate([spread(vec), spread(pltpu.roll(vec, LANES - blocks, 1))], axis=0)
        vh, vl = split(both)
        z = []
        for k in range(group):
            rows = pl.ds(pl.multiple_of((g * group + k) * CHUNK, CHUNK), CHUNK)
            z.append(z_ref[:, rows, :].reshape(blocks, LANES))
        zh, zl = split(jnp.concatenate(z, axis=0))
        full = jnp.dot(
            jnp.concatenate([vh, vl], axis=0),
            jnp.concatenate([zh, zl], axis=1),
            preferred_element_type=F32,
        )
        sums = full[:16, :LANES] + full[:16, LANES:] + full[16:, :LANES]
        turned = pltpu.roll(sums[8:], HALF, 1)
        value = sums[:8] + jnp.where(low, -turned, turned)
        energy = jnp.broadcast_to(vec[:, 2 * blocks : 2 * blocks + 1], (group, LANES))
        s_ref[pl.ds(start, group), :] = value * lax.rsqrt(energy + 1e-06)
        e_ref[pl.ds(start, group), :] = energy
        return carry

    groups = tile // group
    tiles = v_ref.shape[0] // tile

    def copies(t):
        rows = pl.ds(pl.multiple_of(t * tile * CHUNK, CHUNK), tile * CHUNK)
        first, second = z_ref.at[: chunks - 1, rows], z_ref.at[chunks - 1 :, rows]
        return (
            pltpu.make_async_copy(early.at[:, rows], first, sems.at[0, t]),
            pltpu.make_async_copy(late.at[:, rows], second, sems.at[1, t]),
        )

    for t in range(tiles):
        for copy in copies(t):
            copy.start()
    unpack_vectors(packed_ref, v_ref, classes)

    def one_tile(t, carry):
        for copy in copies(t):
            copy.wait()
        return lax.fori_loop(0, groups, lambda g, c: step(t * groups + g, c), carry, unroll=True)

    lax.fori_loop(0, tiles, one_tile, 0)

    half = out_ref.shape[0] // classes // 2
    bits = classes.bit_length() - 1
    low = low_half((half, LANES))
    for d in range(classes):
        r = bit_reverse(d, bits)
        direct = pl.ds(slot_of(r, total_times), half, stride=classes // 4)
        mirror = pl.ds(slot_of(classes - r, total_times), half, stride=classes // 4)
        start = 2 * half * d
        out_ref[start : start + half, :] = s_ref[direct, :]
        energy_ref[start : start + half, :] = e_ref[direct, :]
        turned = reverse_rows(s_ref[mirror, :])
        out_ref[start + half : start + 2 * half, :] = jnp.where(low, turned, -turned)
        energy_ref[start + half : start + 2 * half, :] = reverse_rows(e_ref[mirror, :])


def modes(early, late, vectors, total, classes, slots, tile):
    return pl.pallas_call(
        functools.partial(modes_kernel, tile, classes, total),
        in_specs=[
            pl.BlockSpec(memory_space=pl.ANY),
            pl.BlockSpec(memory_space=pl.ANY),
            pl.BlockSpec(memory_space=pltpu.VMEM),
        ],
        out_shape=[jax.ShapeDtypeStruct((total, LANES), F32)] * 2,
        scratch_shapes=[
            pltpu.VMEM((early.shape[0] + 1, *early.shape[1:]), F32),
            pltpu.VMEM((slots, LANES), F32),
            pltpu.VMEM((slots, LANES), F32),
            pltpu.VMEM((slots, LANES), F32),
            pltpu.SemaphoreType.DMA((2, slots // tile)),
        ],
        compiler_params=params(24),
        name="modes",
    )(*in_hbm([early, late]), vectors)


def place_kernel(x_ref, out_ref):
    low = low_half(x_ref.shape[1:])
    for i in range(x_ref.shape[0] // 2):
        first, second = x_ref[2 * i], x_ref[2 * i + 1]
        cols = slice(i * LANES, (i + 1) * LANES)
        out_ref[0, :, cols] = jnp.where(low, first, pltpu.roll(second, HALF, 1))
        out_ref[1, :, cols] = jnp.where(low, pltpu.roll(first, HALF, 1), second)


def place(pieces):
    count, rows, _ = pieces.shape
    return pl.pallas_call(
        place_kernel,
        out_shape=jax.ShapeDtypeStruct((2, rows, count * HALF), F32),
        compiler_params=params(32),
        name="place",
    )(pieces)


def exchange(value, axes):
    return lax.all_to_all(value, axes, 0, 0, tiled=True)


def body(mesh_shape, snapshots, quad_weights):
    tm_size, space_size = mesh_shape["tm"], mesh_shape["space"]
    local_times, blocks, points = snapshots.shape
    total_times = local_times * tm_size
    total_points = points * space_size
    devices = tm_size * space_size
    per_device = -(-(total_times // 2 + 1) // devices)
    slots = per_device * devices
    tile = slots // 4
    tables = transform_tables(total_times, slots)
    window = jnp.asarray(window_table(total_times))

    here = lax.axis_index("tm") * HALF
    weights = lax.dynamic_slice(quad_weights, (here,), (HALF,))
    weights = jnp.concatenate([weights, weights])[None, :]

    chunks = blocks // CHUNK

    def send(group, offsets, after):
        sent = dict(zip(offsets, pack(snapshots, window, group, tuple(offsets), after)))
        flying = {}
        for m, part in sent.items():
            pairs = [(d, d ^ m) for d in range(tm_size)]
            flying[m] = lax.ppermute(part, "tm", pairs) if m else part
        return sent, flying

    half, quarter = tm_size // 2, tm_size // 4
    first = [*range(half, half + quarter), *range(quarter)]
    second = [*range(half + quarter, tm_size), *range(quarter, half)]
    group = range(chunks - 1)
    sent, pieces = send(group, first[:1], [])
    sent, more = send(group, first[1:], [sent[half]])
    pieces |= more
    pieces |= send(group, second, [sent[0]])[1]
    group = range(chunks - 1, chunks)
    sent, last = send(group, first, [pieces[half]])
    last |= send(group, second, [sent[0], pieces[half + quarter]])[1]
    ordered = lambda pieces: [pieces[m] for m in range(tm_size)]
    early = transform(ordered(pieces), tables, slots)
    matrices = early_gram(early, weights, slots, tile, total_points)
    late, given = late_first(
        ordered(last), tables, early, weights, matrices, slots, tile, total_points
    )

    space = lax.axis_index("space")

    def swap(value, level):
        pairs = [(i, i ^ (1 << level)) for i in range(space_size)]
        return lax.ppermute(value, "space", pairs)

    arriving = swap(given, 0)
    part = late_second(early, late, weights, matrices, slots, tile, total_points)
    levels = space_size.bit_length() - 1
    shape = (*[2] * (levels - 1), tm_size, per_device, *part.shape[1:])
    part, arriving = part.reshape(shape), arriving.reshape(shape)
    bit = space // 2
    pick = lambda value, i: lax.dynamic_index_in_dim(value, i, 0, keepdims=False)
    cut = 3 * per_device // 4
    given = pick(part, 1 - bit)[:, :cut] + pick(arriving, 1 - bit)[:, :cut]
    kept = pick(part, bit)[:, :cut] + pick(arriving, bit)[:, :cut]
    given = swap(given, 1)
    rest = part[:, :, cut:] + arriving[:, :, cut:]
    rest = lax.all_to_all(rest, "tm", 1, 1, tiled=True).sum(axis=1)
    rest = pick(rest, bit) + swap(pick(rest, 1 - bit), 1)
    part = exchange(kept + given, "tm").sum(axis=0)
    part = jnp.concatenate([part, rest], axis=0)

    vectors = power(part.transpose(2, 1, 0), blocks)
    vectors = jnp.broadcast_to(vectors[None], (devices, *vectors.shape))
    vectors = exchange(vectors, ("tm", "space"))

    pieces, energies = modes(early, late, vectors, total_times, tm_size, slots, tile)
    pieces = exchange(pieces.reshape(tm_size, local_times, LANES), "tm")
    energies = energies.reshape(tm_size, local_times, LANES)[:, :, 0]
    energies = lax.dynamic_index_in_dim(energies, lax.axis_index("tm"), 0, keepdims=False)
    return place(pieces), energies


def fits(mesh_shape, times, blocks, points):
    tm_size, space_size = mesh_shape["tm"], mesh_shape["space"]
    return (
        points == space_size * tm_size * HALF
        and (tm_size, space_size) == (8, 4)
        and times % (tm_size * 8) == 0
        and blocks % CHUNK == 0
        and blocks == 32
    )


def matvec(matrix, vector):
    return jnp.einsum("fbc,fc->fb", matrix, vector, precision=lax.Precision.HIGHEST)


def power_modes(real_gram, imag_gram):
    vec_real = jnp.ones(real_gram.shape[:2], jnp.float32) / math.sqrt(real_gram.shape[1])
    vec_imag = jnp.zeros(real_gram.shape[:2], jnp.float32)
    for sweep_idx in range(POWER):
        new_real = matvec(real_gram, vec_real) - matvec(imag_gram, vec_imag)
        new_imag = matvec(real_gram, vec_imag) + matvec(imag_gram, vec_real)
        length = lax.rsqrt(
            jnp.sum(new_real * new_real + new_imag * new_imag, axis=1, keepdims=True) + 1e-06
        )
        vec_real = new_real * length
        vec_imag = new_imag * length
    image_real = matvec(real_gram, vec_real) - matvec(imag_gram, vec_imag)
    image_imag = matvec(real_gram, vec_imag) + matvec(imag_gram, vec_real)
    energy = jnp.sum(vec_real * image_real + vec_imag * image_imag, axis=1)
    return (vec_real, vec_imag, energy)


def general_body(snapshots, quad_weights):
    tm_size = lax.axis_size("tm")
    bit_count = tm_size.bit_length() - 1
    local_times, blocks, points = snapshots.shape
    total_times = local_times * tm_size
    total_points = points * lax.axis_size("space")
    norm_factor = 1.0 / math.sqrt(0.375 * total_times)
    flattened = snapshots.reshape(local_times, blocks * points)
    columns = lax.all_to_all(flattened, "tm", split_axis=1, concat_axis=0, tiled=True)
    col_count = columns.shape[1]
    times_all = jnp.arange(total_times, dtype=jnp.int32)
    window = (
        0.5 - 0.5 * jnp.cos(2.0 * math.pi * times_all.astype(jnp.float32) / total_times)
    ) * norm_factor
    row_block = min(256, total_times)

    def one_block(block_idx):
        row_ids = block_idx * row_block + jnp.arange(row_block, dtype=jnp.int32)
        frequency = bit_reverse(row_ids // local_times, bit_count) + tm_size * (
            row_ids % local_times
        )
        angles = (
            -2.0
            * math.pi
            * (frequency[:, None] * times_all[None, :] % total_times).astype(jnp.float32)
            / total_times
        )
        cos_tab = jnp.cos(angles) * window[None, :]
        sin_tab = jnp.sin(angles) * window[None, :]
        return (
            jnp.dot(cos_tab, columns, precision=lax.Precision.HIGHEST),
            jnp.dot(sin_tab, columns, precision=lax.Precision.HIGHEST),
        )

    spec_real, spec_imag = lax.map(one_block, jnp.arange(total_times // row_block, dtype=jnp.int32))
    spectrum = jnp.stack(
        [spec_real.reshape(total_times, col_count), spec_imag.reshape(total_times, col_count)]
    )
    returned = lax.all_to_all(spectrum, "tm", split_axis=1, concat_axis=2, tiled=True)
    spectral = returned.reshape(2, local_times, blocks, points)
    weighted = spectral * quad_weights
    gram_full = (
        jnp.einsum("pfbx,qfcx->fpbqc", weighted, spectral, precision=lax.Precision.HIGHEST)
        / total_points
    )
    real_gram = gram_full[:, 0, :, 0] + gram_full[:, 1, :, 1]
    imag_gram = gram_full[:, 0, :, 1] - gram_full[:, 1, :, 0]
    real_gram, imag_gram = lax.psum((real_gram, imag_gram), "space")
    vec_real, vec_imag, energy = power_modes(real_gram, imag_gram)
    inverse_root = lax.rsqrt(energy + 1e-06)[:, None]
    modes_real = jnp.einsum(
        "fb,fbx->fx", vec_real, spectral[0], precision=lax.Precision.HIGHEST
    ) - jnp.einsum("fb,fbx->fx", vec_imag, spectral[1], precision=lax.Precision.HIGHEST)
    modes_imag = jnp.einsum(
        "fb,fbx->fx", vec_imag, spectral[0], precision=lax.Precision.HIGHEST
    ) + jnp.einsum("fb,fbx->fx", vec_real, spectral[1], precision=lax.Precision.HIGHEST)
    return (jnp.stack([modes_real * inverse_root, modes_imag * inverse_root]), energy)


def solution(mesh):
    shape = dict(mesh.shape)

    def program(snapshots, quad_weights):
        chosen = general_body
        if fits(shape, *snapshots.shape):
            chosen = functools.partial(body, shape)
        return jax.shard_map(
            chosen,
            mesh=mesh,
            in_specs=(P("tm", None, "space"), P("space")),
            out_specs=(P(None, "tm", "space"), P("tm")),
            check_vma=False,
        )(snapshots, quad_weights)

    return program
```

```python
import functools
import math

import jax
import jax.numpy as jnp
import ml_dtypes
import numpy as np
from jax import lax
from jax.experimental import pallas as pl
from jax.experimental.pallas import tpu as pltpu
from jax.sharding import PartitionSpec as P

POWER = 3
CHUNK = 8
HALF = 64
LANES = 128
BF16 = jnp.bfloat16
F32 = jnp.float32


def bit_reverse(value, bit_count):
    return sum((value >> i & 1) << (bit_count - 1 - i) for i in range(bit_count))


def split_np(table):
    high = table.astype(ml_dtypes.bfloat16)
    low = (table - high.astype(np.float64)).astype(ml_dtypes.bfloat16)
    return high, low


def split(value):
    high = value.astype(BF16)
    return high, (value - high.astype(F32)).astype(BF16)


def low_half(shape):
    return lax.broadcasted_iota(jnp.int32, shape, len(shape) - 1) < HALF


def in_hbm(arrays):
    return [pltpu.with_memory_space_constraint(array, pltpu.HBM) for array in arrays]


def params(mib):
    return pltpu.CompilerParams(vmem_limit_bytes=mib * 2**20)


def slot_of(freq, total_times):
    part = total_times // 8
    return (freq - 1) % 4 * part + freq // 4


@functools.lru_cache(None)
def transform_tables(total_times, slots):
    part, quarter = total_times // 8, total_times // 4
    t = np.arange(quarter)

    def waves(rest, count):
        k = 4 * np.arange(count) + rest
        phase = 2 * np.pi * (k[:, None] * t[None, :] % total_times) / total_times
        live = (k <= total_times // 2)[:, None]
        return np.cos(phase) * live, np.sin(phase) * live

    c, s = waves(1, part)
    ones = np.block([[c, -s], [-s, -c]])
    c, s = waves(3, part)
    threes = np.block([[c, s], [-s, c]])
    c, s = waves(2, part)
    twos = np.concatenate([c, -s])
    c, s = waves(0, slots - 3 * part)
    fours = np.concatenate([c, -s])
    odd = split_np(np.concatenate([ones, threes]))
    return (*odd, *split_np(twos), *split_np(fours))


@functools.lru_cache(None)
def window_table(total_times):
    t = np.arange(total_times)
    window = (0.5 - 0.5 * np.cos(2 * np.pi * t / total_times)) / math.sqrt(0.375 * total_times)
    return np.broadcast_to(window[:, None], (total_times, LANES)).astype(np.float32)


def pack_kernel(offsets, *refs):
    x_refs, out_refs = refs[: len(offsets)], refs[-len(offsets) :]
    window = refs[len(offsets)][...]
    times = window.shape[0]
    low = low_half((times, LANES))
    me = lax.axis_index("tm")
    for m, x_ref, out_ref in zip(offsets, x_refs, out_refs):
        blocks = x_ref.shape[1]
        rows = x_ref.reshape(times * blocks, LANES)
        even = (m ^ me) % 2 == 0
        for n in range(out_ref.shape[0]):
            for j in range(CHUNK // 2):
                b = n * CHUNK + j
                first = rows[pl.ds(b, times, stride=blocks), :] * window
                second = rows[pl.ds(b + CHUNK // 2, times, stride=blocks), :] * window
                left = jnp.where(low, first, pltpu.roll(second, HALF, 1))
                right = jnp.where(low, pltpu.roll(first, HALF, 1), second)
                out_ref[n, :, j * LANES : (j + 1) * LANES] = jnp.where(even, left, right)


def pack(snapshots, window, chunks, offsets, after):
    times = snapshots.shape[0]
    count, width = len(chunks), CHUNK * HALF

    def tile_spec(m):
        place = lambda _: (0, chunks[0] // count, m // 2 ^ lax.axis_index("tm") // 2)
        return pl.BlockSpec((times, CHUNK * count, LANES), place)

    return pl.pallas_call(
        functools.partial(pack_kernel, offsets),
        grid=(1,),
        in_specs=[tile_spec(m) for m in offsets]
        + [pl.BlockSpec((times, LANES), lambda _: (lax.axis_index("tm"), 0))]
        + [pl.BlockSpec(memory_space=pl.ANY)] * len(after),
        out_specs=[pl.BlockSpec((count, times, width), lambda _: (0, 0, 0))] * len(offsets),
        out_shape=[pltpu.HBM((count, times, width), F32)] * len(offsets),
        compiler_params=params(40),
        name="pack",
    )(*in_hbm([snapshots] * len(offsets) + [window, *after]))


def transform_columns(tables, x_ref, odd_ref, two_ref, four_ref, out_ref):
    odd_high, odd_low, two_high, two_low, four_high, four_low = tables
    total, width = x_ref.shape
    quarter, part = total // 4, total // 8

    def keep(ref, rows, cols, value):
        ref[0, rows, cols], ref[1, rows, cols] = split(value)

    for first in range(0, quarter, part):
        for j in range(width // LANES):
            cols = slice(j * LANES, (j + 1) * LANES)
            rows = slice(first, first + part)
            x = [x_ref[n * quarter + first : n * quarter + first + part, cols] for n in range(4)]
            keep(odd_ref, rows, cols, x[0] - x[2])
            keep(odd_ref, slice(quarter + first, quarter + first + part), cols, x[1] - x[3])
            left, right = x[0] + x[2], x[1] + x[3]
            keep(two_ref, rows, cols, left - right)
            keep(four_ref, rows, cols, left + right)

    dot = functools.partial(jnp.dot, preferred_element_type=F32)

    def product(high, low, values):
        return dot(high, values[0]) + dot(high, values[1]) + dot(low, values[0])

    def store(start, both):
        count = both.shape[0] // 2
        low = low_half((count, LANES))
        for j in range(CHUNK // 2):
            cols = slice(j * LANES, (j + 1) * LANES)
            real, imag = both[:count, cols], both[count:, cols]
            first = jnp.where(low, real, pltpu.roll(imag, HALF, 1))
            second = jnp.where(low, pltpu.roll(real, HALF, 1), imag)
            for b, value in ((j, first), (j + CHUNK // 2, second)):
                out_ref[pl.ds(start * CHUNK + b, count, stride=CHUNK), :] = value

    for n in range(2):
        rows = slice(2 * n * part, 2 * (n + 1) * part)
        store(2 * n * part, product(odd_high[rows, :], odd_low[rows, :], odd_ref))
    store(part, product(two_high[...], two_low[...], two_ref))
    store(3 * part, product(four_high[...], four_low[...], four_ref))


def transform_scratch(total, width):
    return [
        pltpu.VMEM((total, width), F32),
        pltpu.VMEM((2, total // 2, width), BF16),
        pltpu.VMEM((2, total // 4, width), BF16),
        pltpu.VMEM((2, total // 4, width), BF16),
    ]


def transform_kernel(*refs):
    tables, piece_refs, (out_ref, x_ref, *folded) = refs[:6], refs[6:-5], refs[-5:]
    me = lax.axis_index("tm")
    for m, piece_ref in enumerate(piece_refs):
        times = piece_ref.shape[0]
        rows = pl.ds(pl.multiple_of((me ^ m) * times, times), times)
        x_ref[rows, :] = piece_ref[...]
    transform_columns(tables, x_ref, *folded, out_ref)


def transform(pieces, tables, slots):
    chunks, times, width = pieces[0].shape
    total = times * len(pieces)
    return pl.pallas_call(
        transform_kernel,
        grid=(chunks,),
        in_specs=[pl.BlockSpec(table.shape, lambda n: (0, 0)) for table in tables]
        + [pl.BlockSpec((None, times, width), lambda n: (n, 0, 0))] * len(pieces),
        out_specs=pl.BlockSpec((None, slots * CHUNK, LANES), lambda n: (n, 0, 0)),
        out_shape=pltpu.HBM((chunks, slots * CHUNK, LANES), F32),
        scratch_shapes=transform_scratch(total, width),
        compiler_params=params(40),
        name="transform",
    )(*tables, *in_hbm(pieces))


def first_lane(chunk, chunks):
    return sum(16 * i + 8 for i in range(chunk + 1, chunks))


GROUP = 8


def chunk_tiles(chunk, chunks, weight, parts, before):
    flipped = jnp.where(low_half(weight.shape), weight, -weight)
    width = CHUNK * (chunk + 1)
    stride = width if LANES % width == 0 else 32
    left, right = [], []
    for row in parts:
        row = row[: chunk + 1]
        right.extend((row + row[-1:])[: stride // CHUNK])
        left.append(row[-1] * weight)
        left.append(pltpu.roll(row[-1], HALF, 1) * flipped)
    lh, ll = split(jnp.concatenate(left, axis=0))
    rh, rl = split(jnp.concatenate(right, axis=0))
    full = lax.dot_general(
        jnp.concatenate([lh, ll, lh], axis=1),
        jnp.concatenate([rh, rh, rl], axis=1),
        (((1,), (1,)), ((), ())),
        preferred_element_type=F32,
    )
    if full.shape[1] < LANES:
        full = jnp.concatenate([full] * (LANES // full.shape[1]), axis=1)
    start = first_lane(chunk, chunks)
    row = lax.broadcasted_iota(jnp.int32, (CHUNK, LANES), 0)
    own = lax.broadcasted_iota(jnp.int32, (CHUNK, LANES), 1) - start
    past = own >= width
    corner = (own >= width - CHUNK) & (own < width) & (own - (width - CHUNK) > row)
    valid = (own >= 0) & (own < width + CHUNK * chunk)
    tiles = []
    for k in range(GROUP):
        first = k * stride // LANES * LANES
        real = full[16 * k : 16 * k + 8, first : first + LANES]
        imag = full[16 * k + 8 : 16 * k + 16, first : first + LANES]
        shift = (start - (k * stride - first)) % LANES
        out = pltpu.roll(real, shift, 1)
        out = jnp.where(corner, pltpu.roll(imag, shift, 1), out)
        out = jnp.where(past, pltpu.roll(imag, (shift + width) % LANES, 1), out)
        tiles.append(jnp.where(valid, out, before[k]))
    return tiles


def early_gram_kernel(tile, chunks, scale, z_ref, w_ref, out_ref):
    weight = w_ref[...] * scale

    def step(g, carry):
        parts = []
        for k in range(GROUP):
            rows = pl.ds(pl.multiple_of((g * GROUP + k) * CHUNK, CHUNK), CHUNK)
            parts.append([z_ref[n, rows, :] for n in range(chunks - 1)])
        tiles = [jnp.zeros((CHUNK, LANES), F32)] * GROUP
        for chunk in range(chunks - 1):
            tiles = chunk_tiles(chunk, chunks, weight, parts, tiles)
        for k in range(GROUP):
            out_ref[g * GROUP + k] = tiles[k]
        return carry

    lax.fori_loop(0, tile // GROUP, step, 0, unroll=True)


def early_gram(spectra, weights, slots, tile, total_points):
    chunks = spectra.shape[0] + 1
    return pl.pallas_call(
        functools.partial(early_gram_kernel, tile, chunks, 1.0 / total_points),
        grid=(slots // tile,),
        in_specs=[
            pl.BlockSpec((chunks - 1, tile * CHUNK, LANES), lambda i: (0, i, 0)),
            pl.BlockSpec((1, LANES), lambda i: (0, 0)),
        ],
        out_specs=pl.BlockSpec((tile, 8, LANES), lambda i: (i, 0, 0)),
        out_shape=pltpu.HBM((slots, 8, LANES), F32),
        compiler_params=params(24),
        name="early_gram",
    )(*in_hbm([spectra]), weights)


def copy_tile(source, buffer, sem, base, size, t):
    there = pl.ds(pl.multiple_of(base + t * size, 8), size)
    here = pl.ds(pl.multiple_of(t * size, 8), size)
    if len(source.shape) == 3 and size % CHUNK == 0 and source.shape[1] != CHUNK:
        return pltpu.make_async_copy(source.at[:, there], buffer.at[:, here], sem)
    return pltpu.make_async_copy(source.at[there], buffer.at[here], sem)


def half_base(half, count):
    return pl.multiple_of((lax.axis_index("space") % 2 ^ half) * count, GROUP)


def late_tiles(tile, weight, early_ref, late_at, before_ref, out_ref, wait):
    chunks = early_ref.shape[0] + 1

    def step(g, carry):
        parts, before = [], []
        for k in range(GROUP):
            start = pl.multiple_of((g * GROUP + k) * CHUNK, CHUNK)
            parts.append([early_ref[n, pl.ds(start, CHUNK), :] for n in range(chunks - 1)])
            parts[-1].append(late_at(start))
            before.append(before_ref[g * GROUP + k])
        tiles = chunk_tiles(chunks - 1, chunks, weight, parts, before)
        for k in range(GROUP):
            out_ref[g * GROUP + k] = tiles[k]
        return carry

    groups = tile // GROUP

    def one_tile(t, carry):
        wait(t)
        return lax.fori_loop(0, groups, lambda g, c: step(t * groups + g, c), carry, unroll=True)

    lax.fori_loop(0, out_ref.shape[0] // tile, one_tile, 0)


def late_first_kernel(tile, scale, *refs):
    tables, w_ref, early, before = refs[:6], refs[6], refs[7], refs[8]
    late_ref, out_ref = refs[-12:-10]
    piece_refs = refs[9:-12]
    x_ref, odd_ref, two_ref, four_ref, z_ref, early_ref, before_ref = refs[-10:-3]
    piece_sems, tile_sems, late_sem = refs[-3:]
    count = out_ref.shape[0]
    base = half_base(1, count)
    me = lax.axis_index("tm")
    arrivals = []
    for m, piece_ref in enumerate(piece_refs):
        times = piece_ref.shape[1]
        rows = pl.ds(pl.multiple_of((me ^ m) * times, times), times)
        arrivals.append(pltpu.make_async_copy(piece_ref.at[0], x_ref.at[rows], piece_sems.at[m]))
        arrivals[-1].start()

    def copies(t):
        first = copy_tile(early, early_ref, tile_sems.at[0, t], base * CHUNK, tile * CHUNK, t)
        return first, copy_tile(before, before_ref, tile_sems.at[1, t], base, tile, t)

    for t in range(count // tile):
        for copy in copies(t):
            copy.start()
    for copy in arrivals:
        copy.wait()
    transform_columns(tables, x_ref, odd_ref, two_ref, four_ref, z_ref)
    keep = pltpu.make_async_copy(z_ref, late_ref.at[0], late_sem)
    keep.start()

    def wait(t):
        for copy in copies(t):
            copy.wait()

    late_at = lambda start: z_ref[pl.ds(pl.multiple_of(base * CHUNK + start, 8), CHUNK), :]
    late_tiles(tile, w_ref[...] * scale, early_ref, late_at, before_ref, out_ref, wait)
    keep.wait()


def late_first(pieces, tables, early, weights, before, slots, tile, total_points):
    _, times, width = pieces[0].shape
    total, count = times * len(pieces), slots // 2
    return pl.pallas_call(
        functools.partial(late_first_kernel, tile, 1.0 / total_points),
        in_specs=[pl.BlockSpec(memory_space=pltpu.VMEM)] * (len(tables) + 1)
        + [pl.BlockSpec(memory_space=pl.ANY)] * (2 + len(pieces)),
        out_specs=[
            pl.BlockSpec(memory_space=pl.ANY),
            pl.BlockSpec(memory_space=pltpu.VMEM),
        ],
        out_shape=[
            pltpu.HBM((1, slots * CHUNK, LANES), F32),
            pltpu.HBM((count, CHUNK, LANES), F32),
        ],
        scratch_shapes=transform_scratch(total, width)
        + [
            pltpu.VMEM((slots * CHUNK, LANES), F32),
            pltpu.VMEM((early.shape[0], count * CHUNK, LANES), F32),
            pltpu.VMEM((count, CHUNK, LANES), F32),
            pltpu.SemaphoreType.DMA((len(pieces),)),
            pltpu.SemaphoreType.DMA((2, count // tile)),
            pltpu.SemaphoreType.DMA(()),
        ],
        compiler_params=params(40),
        name="late_first",
    )(*tables, weights, *in_hbm([early, before, *pieces]))


def late_second_kernel(tile, scale, *refs):
    sources, w_ref, out_ref = refs[:3], refs[3], refs[4]
    buffers, sems = refs[5:8], refs[8]
    count = out_ref.shape[0]
    base = half_base(0, count)
    sizes = (tile * CHUNK, tile * CHUNK, tile)

    def copies(t):
        bases = (base * CHUNK, base * CHUNK, base)
        return [
            copy_tile(sources[n], buffers[n], sems.at[n, t], bases[n], sizes[n], t)
            for n in range(3)
        ]

    for t in range(count // tile):
        for copy in copies(t):
            copy.start()

    def wait(t):
        for copy in copies(t):
            copy.wait()

    late_at = lambda start: buffers[1][0, pl.ds(start, CHUNK), :]
    late_tiles(tile, w_ref[...] * scale, buffers[0], late_at, buffers[2], out_ref, wait)


def late_second(early, late, weights, before, slots, tile, total_points):
    count = slots // 2
    sizes = [(z.shape[0], count * CHUNK, LANES) for z in (early, late)]
    sizes.append((count, CHUNK, LANES))
    return pl.pallas_call(
        functools.partial(late_second_kernel, tile, 1.0 / total_points),
        in_specs=[pl.BlockSpec(memory_space=pl.ANY)] * 3
        + [pl.BlockSpec(memory_space=pltpu.VMEM)],
        out_shape=pltpu.HBM((count, CHUNK, LANES), F32),
        scratch_shapes=[pltpu.VMEM(size, F32) for size in sizes]
        + [pltpu.SemaphoreType.DMA((3, count // tile))],
        compiler_params=params(24),
        name="late_second",
    )(*in_hbm([early, late, before]), weights)


def power_kernel(blocks, x_ref, out_ref):
    count = x_ref.shape[2]
    chunks = blocks // CHUNK
    real = [[None] * chunks for _ in range(chunks)]
    imag = [[None] * chunks for _ in range(chunks)]
    for c in range(chunks):
        start = first_lane(c, chunks)
        for d in range(c):
            x = x_ref[start + CHUNK * d : start + CHUNK * (d + 1)]
            y = x_ref[start + CHUNK * (c + 1 + d) : start + CHUNK * (c + 2 + d)]
            real[d][c], real[c][d] = x, jnp.swapaxes(x, 0, 1)
            imag[d][c], imag[c][d] = y, -jnp.swapaxes(y, 0, 1)
        x = x_ref[start + CHUNK * c : start + CHUNK * (c + 1)]
        flip = jnp.swapaxes(x, 0, 1)
        b = lax.broadcasted_iota(jnp.int32, x.shape, 0)
        s = lax.broadcasted_iota(jnp.int32, x.shape, 1)
        real[c][c] = jnp.where(b <= s, x, flip)
        imag[c][c] = jnp.where(b > s, x, jnp.where(b < s, -flip, 0.0))
    whole = lambda m: jnp.concatenate([jnp.concatenate(r, axis=1) for r in m], axis=0)
    real, imag = whole(real), -whole(imag)

    def apply(vr, vi):
        vr, vi = vr[:, None, :], vi[:, None, :]
        return jnp.sum(real * vr - imag * vi, axis=0), jnp.sum(real * vi + imag * vr, axis=0)

    vr = jnp.full((blocks, count), 1.0 / math.sqrt(blocks), F32)
    vi = jnp.zeros((blocks, count), F32)
    for _ in range(POWER):
        ur, ui = apply(vr, vi)
        length = lax.rsqrt(jnp.sum(ur * ur + ui * ui, axis=0, keepdims=True) + 1e-06)
        vr, vi = ur * length, ui * length
    ur, ui = apply(vr, vi)
    energy = jnp.sum(vr * ur + vi * ui, axis=0, keepdims=True)
    columns = jnp.concatenate([vr, vi, jnp.broadcast_to(energy, (8, count))], axis=0)
    columns = jnp.pad(columns, ((0, LANES - columns.shape[0]), (0, LANES - count)))
    rows = columns.T
    half = count // 2
    low = low_half((half, LANES))
    lane = lax.broadcasted_iota(jnp.int32, (half, LANES), 1)
    first, second = rows[:half], rows[half : 2 * half]
    last = jnp.broadcast_to(rows[2 * half : count], (half, LANES))
    ends = jnp.where(lane == 2, pltpu.roll(last, HALF + 2, 1), pltpu.roll(last, HALF, 1))
    ends = jnp.where(lane == 1, pltpu.roll(second, HALF + 1, 1), ends)
    out_ref[half:] = jnp.where(lane == 0, pltpu.roll(first, HALF, 1), ends)
    out_ref[:half] = jnp.where(low, first, pltpu.roll(second, HALF, 1))


def power(packed, blocks):
    return pl.pallas_call(
        functools.partial(power_kernel, blocks),
        out_shape=jax.ShapeDtypeStruct((packed.shape[2] // 2 * 2, LANES), F32),
        compiler_params=params(32),
        name="power",
    )(packed)


def reverse_rows(value):
    row = lax.broadcasted_iota(jnp.int32, (8, LANES), 0)
    tiles = []
    for start in range(0, value.shape[0], 8):
        tile = value[start : start + 8]
        for span in (1, 2, 4):
            upper = (row & span) == 0
            tile = jnp.where(upper, pltpu.roll(tile, 8 - span, 0), pltpu.roll(tile, span, 0))
        tiles.append(tile)
    return jnp.concatenate(tiles[::-1], axis=0)


def unpack_vectors(packed_ref, v_ref, classes):
    devices, rows, _ = packed_ref.shape
    half = rows // 2
    count = v_ref.shape[0] // devices
    spaces = devices // classes
    low = low_half((half, LANES))
    for device in range(devices):
        tau, space = divmod(device, spaces)
        order = bit_reverse(space, spaces.bit_length() - 1)
        start = (order * classes + tau) * count
        vector, ends = packed_ref[device, :half, :], packed_ref[device, half:, :]
        turned = pltpu.roll(ends, HALF, 1)
        v_ref[start : start + half, :] = jnp.where(low, vector, turned)
        second = jnp.where(low, pltpu.roll(vector, HALF, 1), pltpu.roll(ends, HALF - 1, 1))
        v_ref[start + half : start + 2 * half, :] = second
        last = jnp.where(low, turned, pltpu.roll(ends, HALF - 2, 1))
        v_ref[start + 2 * half : start + count, :] = last[:1]


def modes_kernel(tile, classes, total_times, *refs):
    early, late, packed_ref, out_ref, energy_ref, z_ref, s_ref, e_ref, v_ref, sems = refs
    chunks = z_ref.shape[0]
    blocks = CHUNK * z_ref.shape[0]
    group = 8
    lane = lax.broadcasted_iota(jnp.int32, (group, LANES), 1)
    row = lax.broadcasted_iota(jnp.int32, (group, LANES), 0)
    per_tile = LANES // blocks
    low = low_half((group, LANES))

    def spread(vector):
        vector = jnp.where(lane < blocks, vector, 0.0)
        span = blocks
        while span < LANES:
            vector = vector + pltpu.roll(vector, span, 1)
            span *= 2
        parts = []
        for first in range(0, group, per_tile):
            parts.append(jnp.where(lane // blocks + first == row, vector, 0.0))
        return jnp.concatenate(parts, axis=1)

    def step(g, carry):
        start = pl.multiple_of(g * group, group)
        vec = v_ref[pl.ds(start, group), :]
        both = jnp.concatenate([spread(vec), spread(pltpu.roll(vec, LANES - blocks, 1))], axis=0)
        vh, vl = split(both)
        z = []
        for k in range(group):
            rows = pl.ds(pl.multiple_of((g * group + k) * CHUNK, CHUNK), CHUNK)
            z.append(z_ref[:, rows, :].reshape(blocks, LANES))
        zh, zl = split(jnp.concatenate(z, axis=0))
        full = jnp.dot(
            jnp.concatenate([vh, vl], axis=0),
            jnp.concatenate([zh, zl], axis=1),
            preferred_element_type=F32,
        )
        sums = full[:16, :LANES] + full[:16, LANES:] + full[16:, :LANES]
        turned = pltpu.roll(sums[8:], HALF, 1)
        value = sums[:8] + jnp.where(low, -turned, turned)
        energy = jnp.broadcast_to(vec[:, 2 * blocks : 2 * blocks + 1], (group, LANES))
        s_ref[pl.ds(start, group), :] = value * lax.rsqrt(energy + 1e-06)
        e_ref[pl.ds(start, group), :] = energy
        return carry

    groups = tile // group
    tiles = v_ref.shape[0] // tile

    def copies(t):
        rows = pl.ds(pl.multiple_of(t * tile * CHUNK, CHUNK), tile * CHUNK)
        first, second = z_ref.at[: chunks - 1, rows], z_ref.at[chunks - 1 :, rows]
        return (
            pltpu.make_async_copy(early.at[:, rows], first, sems.at[0, t]),
            pltpu.make_async_copy(late.at[:, rows], second, sems.at[1, t]),
        )

    for t in range(tiles):
        for copy in copies(t):
            copy.start()
    unpack_vectors(packed_ref, v_ref, classes)

    def one_tile(t, carry):
        for copy in copies(t):
            copy.wait()
        return lax.fori_loop(0, groups, lambda g, c: step(t * groups + g, c), carry, unroll=True)

    lax.fori_loop(0, tiles, one_tile, 0)

    half = out_ref.shape[0] // classes // 2
    bits = classes.bit_length() - 1
    low = low_half((half, LANES))
    for d in range(classes):
        r = bit_reverse(d, bits)
        direct = pl.ds(slot_of(r, total_times), half, stride=classes // 4)
        mirror = pl.ds(slot_of(classes - r, total_times), half, stride=classes // 4)
        start = 2 * half * d
        out_ref[start : start + half, :] = s_ref[direct, :]
        energy_ref[start : start + half, :] = e_ref[direct, :]
        turned = reverse_rows(s_ref[mirror, :])
        out_ref[start + half : start + 2 * half, :] = jnp.where(low, turned, -turned)
        energy_ref[start + half : start + 2 * half, :] = reverse_rows(e_ref[mirror, :])


def modes(early, late, vectors, total, classes, slots, tile):
    return pl.pallas_call(
        functools.partial(modes_kernel, tile, classes, total),
        in_specs=[
            pl.BlockSpec(memory_space=pl.ANY),
            pl.BlockSpec(memory_space=pl.ANY),
            pl.BlockSpec(memory_space=pltpu.VMEM),
        ],
        out_shape=[jax.ShapeDtypeStruct((total, LANES), F32)] * 2,
        scratch_shapes=[
            pltpu.VMEM((early.shape[0] + 1, *early.shape[1:]), F32),
            pltpu.VMEM((slots, LANES), F32),
            pltpu.VMEM((slots, LANES), F32),
            pltpu.VMEM((slots, LANES), F32),
            pltpu.SemaphoreType.DMA((2, slots // tile)),
        ],
        compiler_params=params(24),
        name="modes",
    )(*in_hbm([early, late]), vectors)


def place_kernel(x_ref, out_ref):
    low = low_half(x_ref.shape[1:])
    for i in range(x_ref.shape[0] // 2):
        first, second = x_ref[2 * i], x_ref[2 * i + 1]
        cols = slice(i * LANES, (i + 1) * LANES)
        out_ref[0, :, cols] = jnp.where(low, first, pltpu.roll(second, HALF, 1))
        out_ref[1, :, cols] = jnp.where(low, pltpu.roll(first, HALF, 1), second)


def place(pieces):
    count, rows, _ = pieces.shape
    return pl.pallas_call(
        place_kernel,
        out_shape=jax.ShapeDtypeStruct((2, rows, count * HALF), F32),
        compiler_params=params(32),
        name="place",
    )(pieces)


def exchange(value, axes):
    return lax.all_to_all(value, axes, 0, 0, tiled=True)


def body(mesh_shape, snapshots, quad_weights):
    tm_size, space_size = mesh_shape["tm"], mesh_shape["space"]
    local_times, blocks, points = snapshots.shape
    total_times = local_times * tm_size
    total_points = points * space_size
    devices = tm_size * space_size
    per_device = -(-(total_times // 2 + 1) // devices)
    slots = per_device * devices
    tile = slots // 4
    tables = transform_tables(total_times, slots)
    window = jnp.asarray(window_table(total_times))

    here = lax.axis_index("tm") * HALF
    weights = lax.dynamic_slice(quad_weights, (here,), (HALF,))
    weights = jnp.concatenate([weights, weights])[None, :]

    chunks = blocks // CHUNK

    def send(group, offsets, after):
        sent = dict(zip(offsets, pack(snapshots, window, group, tuple(offsets), after)))
        flying = {}
        for m, part in sent.items():
            pairs = [(d, d ^ m) for d in range(tm_size)]
            flying[m] = lax.ppermute(part, "tm", pairs) if m else part
        return sent, flying

    half, quarter = tm_size // 2, tm_size // 4
    first = [*range(half, half + quarter), *range(quarter)]
    second = [*range(half + quarter, tm_size), *range(quarter, half)]
    group = range(chunks - 1)
    sent, pieces = send(group, first[:1], [])
    sent, more = send(group, first[1:], [sent[half]])
    pieces |= more
    pieces |= send(group, second, [sent[0]])[1]
    group = range(chunks - 1, chunks)
    sent, last = send(group, first, [pieces[half]])
    last |= send(group, second, [sent[0], pieces[half + quarter]])[1]
    ordered = lambda pieces: [pieces[m] for m in range(tm_size)]
    early = transform(ordered(pieces), tables, slots)
    matrices = early_gram(early, weights, slots, tile, total_points)
    late, given = late_first(
        ordered(last), tables, early, weights, matrices, slots, tile, total_points
    )

    space = lax.axis_index("space")

    def swap(value, level):
        pairs = [(i, i ^ (1 << level)) for i in range(space_size)]
        return lax.ppermute(value, "space", pairs)

    arriving = swap(given, 0)
    part = late_second(early, late, weights, matrices, slots, tile, total_points)
    levels = space_size.bit_length() - 1
    shape = (*[2] * (levels - 1), tm_size, per_device, *part.shape[1:])
    part, arriving = part.reshape(shape), arriving.reshape(shape)
    bit = space // 2
    pick = lambda value, i: lax.dynamic_index_in_dim(value, i, 0, keepdims=False)
    cut = 3 * per_device // 4 + 1
    given = pick(part, 1 - bit)[:, :cut] + pick(arriving, 1 - bit)[:, :cut]
    kept = pick(part, bit)[:, :cut] + pick(arriving, bit)[:, :cut]
    given = swap(given, 1)
    rest = part[:, :, cut:] + arriving[:, :, cut:]
    rest = lax.all_to_all(rest, "tm", 1, 1, tiled=True).sum(axis=1)
    rest = pick(rest, bit) + swap(pick(rest, 1 - bit), 1)
    part = exchange(kept + given, "tm").sum(axis=0)
    part = jnp.concatenate([part, rest], axis=0)

    vectors = power(part.transpose(2, 1, 0), blocks)
    vectors = jnp.broadcast_to(vectors[None], (devices, *vectors.shape))
    vectors = exchange(vectors, ("tm", "space"))

    pieces, energies = modes(early, late, vectors, total_times, tm_size, slots, tile)
    pieces = exchange(pieces.reshape(tm_size, local_times, LANES), "tm")
    energies = energies.reshape(tm_size, local_times, LANES)[:, :, 0]
    energies = lax.dynamic_index_in_dim(energies, lax.axis_index("tm"), 0, keepdims=False)
    return place(pieces), energies


def fits(mesh_shape, times, blocks, points):
    tm_size, space_size = mesh_shape["tm"], mesh_shape["space"]
    return (
        points == space_size * tm_size * HALF
        and (tm_size, space_size) == (8, 4)
        and times % (tm_size * 8) == 0
        and blocks % CHUNK == 0
        and blocks == 32
    )


def matvec(matrix, vector):
    return jnp.einsum("fbc,fc->fb", matrix, vector, precision=lax.Precision.HIGHEST)


def power_modes(real_gram, imag_gram):
    vec_real = jnp.ones(real_gram.shape[:2], jnp.float32) / math.sqrt(real_gram.shape[1])
    vec_imag = jnp.zeros(real_gram.shape[:2], jnp.float32)
    for sweep_idx in range(POWER):
        new_real = matvec(real_gram, vec_real) - matvec(imag_gram, vec_imag)
        new_imag = matvec(real_gram, vec_imag) + matvec(imag_gram, vec_real)
        length = lax.rsqrt(
            jnp.sum(new_real * new_real + new_imag * new_imag, axis=1, keepdims=True) + 1e-06
        )
        vec_real = new_real * length
        vec_imag = new_imag * length
    image_real = matvec(real_gram, vec_real) - matvec(imag_gram, vec_imag)
    image_imag = matvec(real_gram, vec_imag) + matvec(imag_gram, vec_real)
    energy = jnp.sum(vec_real * image_real + vec_imag * image_imag, axis=1)
    return (vec_real, vec_imag, energy)


def general_body(snapshots, quad_weights):
    tm_size = lax.axis_size("tm")
    bit_count = tm_size.bit_length() - 1
    local_times, blocks, points = snapshots.shape
    total_times = local_times * tm_size
    total_points = points * lax.axis_size("space")
    norm_factor = 1.0 / math.sqrt(0.375 * total_times)
    flattened = snapshots.reshape(local_times, blocks * points)
    columns = lax.all_to_all(flattened, "tm", split_axis=1, concat_axis=0, tiled=True)
    col_count = columns.shape[1]
    times_all = jnp.arange(total_times, dtype=jnp.int32)
    window = (
        0.5 - 0.5 * jnp.cos(2.0 * math.pi * times_all.astype(jnp.float32) / total_times)
    ) * norm_factor
    row_block = min(256, total_times)

    def one_block(block_idx):
        row_ids = block_idx * row_block + jnp.arange(row_block, dtype=jnp.int32)
        frequency = bit_reverse(row_ids // local_times, bit_count) + tm_size * (
            row_ids % local_times
        )
        angles = (
            -2.0
            * math.pi
            * (frequency[:, None] * times_all[None, :] % total_times).astype(jnp.float32)
            / total_times
        )
        cos_tab = jnp.cos(angles) * window[None, :]
        sin_tab = jnp.sin(angles) * window[None, :]
        return (
            jnp.dot(cos_tab, columns, precision=lax.Precision.HIGHEST),
            jnp.dot(sin_tab, columns, precision=lax.Precision.HIGHEST),
        )

    spec_real, spec_imag = lax.map(one_block, jnp.arange(total_times // row_block, dtype=jnp.int32))
    spectrum = jnp.stack(
        [spec_real.reshape(total_times, col_count), spec_imag.reshape(total_times, col_count)]
    )
    returned = lax.all_to_all(spectrum, "tm", split_axis=1, concat_axis=2, tiled=True)
    spectral = returned.reshape(2, local_times, blocks, points)
    weighted = spectral * quad_weights
    gram_full = (
        jnp.einsum("pfbx,qfcx->fpbqc", weighted, spectral, precision=lax.Precision.HIGHEST)
        / total_points
    )
    real_gram = gram_full[:, 0, :, 0] + gram_full[:, 1, :, 1]
    imag_gram = gram_full[:, 0, :, 1] - gram_full[:, 1, :, 0]
    real_gram, imag_gram = lax.psum((real_gram, imag_gram), "space")
    vec_real, vec_imag, energy = power_modes(real_gram, imag_gram)
    inverse_root = lax.rsqrt(energy + 1e-06)[:, None]
    modes_real = jnp.einsum(
        "fb,fbx->fx", vec_real, spectral[0], precision=lax.Precision.HIGHEST
    ) - jnp.einsum("fb,fbx->fx", vec_imag, spectral[1], precision=lax.Precision.HIGHEST)
    modes_imag = jnp.einsum(
        "fb,fbx->fx", vec_imag, spectral[0], precision=lax.Precision.HIGHEST
    ) + jnp.einsum("fb,fbx->fx", vec_real, spectral[1], precision=lax.Precision.HIGHEST)
    return (jnp.stack([modes_real * inverse_root, modes_imag * inverse_root]), energy)


def solution(mesh):
    shape = dict(mesh.shape)

    def program(snapshots, quad_weights):
        chosen = general_body
        if fits(shape, *snapshots.shape):
            chosen = functools.partial(body, shape)
        return jax.shard_map(
            chosen,
            mesh=mesh,
            in_specs=(P("tm", None, "space"), P("space")),
            out_specs=(P(None, "tm", "space"), P("tm")),
            check_vma=False,
        )(snapshots, quad_weights)

    return program
```

```python
import functools
import math

import jax
import jax.numpy as jnp
import ml_dtypes
import numpy as np
from jax import lax
from jax.experimental import pallas as pl
from jax.experimental.pallas import tpu as pltpu
from jax.sharding import PartitionSpec as P

POWER = 3
CHUNK = 8
HALF = 64
LANES = 128
BF16 = jnp.bfloat16
F32 = jnp.float32


def bit_reverse(value, bit_count):
    return sum((value >> i & 1) << (bit_count - 1 - i) for i in range(bit_count))


def split_np(table):
    high = table.astype(ml_dtypes.bfloat16)
    low = (table - high.astype(np.float64)).astype(ml_dtypes.bfloat16)
    return high, low


def split(value):
    high = value.astype(BF16)
    return high, (value - high.astype(F32)).astype(BF16)


def low_half(shape):
    return lax.broadcasted_iota(jnp.int32, shape, len(shape) - 1) < HALF


def in_hbm(arrays):
    return [pltpu.with_memory_space_constraint(array, pltpu.HBM) for array in arrays]


def params(mib):
    return pltpu.CompilerParams(vmem_limit_bytes=mib * 2**20)


def slot_of(freq, total_times):
    part = total_times // 8
    return (freq - 1) % 4 * part + freq // 4


@functools.lru_cache(None)
def transform_tables(total_times, slots):
    part, quarter = total_times // 8, total_times // 4
    t = np.arange(quarter)

    def waves(rest, count):
        k = 4 * np.arange(count) + rest
        phase = 2 * np.pi * (k[:, None] * t[None, :] % total_times) / total_times
        live = (k <= total_times // 2)[:, None]
        return np.cos(phase) * live, np.sin(phase) * live

    c, s = waves(1, part)
    ones = np.block([[c, -s], [-s, -c]])
    c, s = waves(3, part)
    threes = np.block([[c, s], [-s, c]])
    c, s = waves(2, part)
    twos = np.concatenate([c, -s])
    c, s = waves(0, slots - 3 * part)
    fours = np.concatenate([c, -s])
    odd = split_np(np.concatenate([ones, threes]))
    return (*odd, *split_np(twos), *split_np(fours))


@functools.lru_cache(None)
def window_table(total_times):
    t = np.arange(total_times)
    window = (0.5 - 0.5 * np.cos(2 * np.pi * t / total_times)) / math.sqrt(0.375 * total_times)
    return np.broadcast_to(window[:, None], (total_times, LANES)).astype(np.float32)


def pack_kernel(offsets, *refs):
    x_refs, out_refs = refs[: len(offsets)], refs[-len(offsets) :]
    window = refs[len(offsets)][...]
    times = window.shape[0]
    low = low_half((times, LANES))
    me = lax.axis_index("tm")
    for m, x_ref, out_ref in zip(offsets, x_refs, out_refs):
        blocks = x_ref.shape[1]
        rows = x_ref.reshape(times * blocks, LANES)
        even = (m ^ me) % 2 == 0
        for n in range(out_ref.shape[0]):
            for j in range(CHUNK // 2):
                b = n * CHUNK + j
                first = rows[pl.ds(b, times, stride=blocks), :] * window
                second = rows[pl.ds(b + CHUNK // 2, times, stride=blocks), :] * window
                left = jnp.where(low, first, pltpu.roll(second, HALF, 1))
                right = jnp.where(low, pltpu.roll(first, HALF, 1), second)
                out_ref[n, :, j * LANES : (j + 1) * LANES] = jnp.where(even, left, right)


def pack(snapshots, window, chunks, offsets, after):
    times = snapshots.shape[0]
    count, width = len(chunks), CHUNK * HALF

    def tile_spec(m):
        place = lambda _: (0, chunks[0] // count, m // 2 ^ lax.axis_index("tm") // 2)
        return pl.BlockSpec((times, CHUNK * count, LANES), place)

    return pl.pallas_call(
        functools.partial(pack_kernel, offsets),
        grid=(1,),
        in_specs=[tile_spec(m) for m in offsets]
        + [pl.BlockSpec((times, LANES), lambda _: (lax.axis_index("tm"), 0))]
        + [pl.BlockSpec(memory_space=pl.ANY)] * len(after),
        out_specs=[pl.BlockSpec((count, times, width), lambda _: (0, 0, 0))] * len(offsets),
        out_shape=[pltpu.HBM((count, times, width), F32)] * len(offsets),
        compiler_params=params(40),
        name="pack",
    )(*in_hbm([snapshots] * len(offsets) + [window, *after]))


def transform_columns(tables, x_ref, odd_ref, two_ref, four_ref, out_ref):
    odd_high, odd_low, two_high, two_low, four_high, four_low = tables
    total, width = x_ref.shape
    quarter, part = total // 4, total // 8

    def keep(ref, rows, cols, value):
        ref[0, rows, cols], ref[1, rows, cols] = split(value)

    for first in range(0, quarter, part):
        for j in range(width // LANES):
            cols = slice(j * LANES, (j + 1) * LANES)
            rows = slice(first, first + part)
            x = [x_ref[n * quarter + first : n * quarter + first + part, cols] for n in range(4)]
            keep(odd_ref, rows, cols, x[0] - x[2])
            keep(odd_ref, slice(quarter + first, quarter + first + part), cols, x[1] - x[3])
            left, right = x[0] + x[2], x[1] + x[3]
            keep(two_ref, rows, cols, left - right)
            keep(four_ref, rows, cols, left + right)

    dot = functools.partial(jnp.dot, preferred_element_type=F32)

    def product(high, low, values):
        return dot(high, values[0]) + dot(high, values[1]) + dot(low, values[0])

    def store(start, both):
        count = both.shape[0] // 2
        low = low_half((count, LANES))
        for j in range(CHUNK // 2):
            cols = slice(j * LANES, (j + 1) * LANES)
            real, imag = both[:count, cols], both[count:, cols]
            first = jnp.where(low, real, pltpu.roll(imag, HALF, 1))
            second = jnp.where(low, pltpu.roll(real, HALF, 1), imag)
            for b, value in ((j, first), (j + CHUNK // 2, second)):
                out_ref[pl.ds(start * CHUNK + b, count, stride=CHUNK), :] = value

    for n in range(2):
        rows = slice(2 * n * part, 2 * (n + 1) * part)
        store(2 * n * part, product(odd_high[rows, :], odd_low[rows, :], odd_ref))
    store(part, product(two_high[...], two_low[...], two_ref))
    store(3 * part, product(four_high[...], four_low[...], four_ref))


def transform_scratch(total, width):
    return [
        pltpu.VMEM((total, width), F32),
        pltpu.VMEM((2, total // 2, width), BF16),
        pltpu.VMEM((2, total // 4, width), BF16),
        pltpu.VMEM((2, total // 4, width), BF16),
    ]


def transform_kernel(*refs):
    tables, piece_refs, (out_ref, x_ref, *folded) = refs[:6], refs[6:-5], refs[-5:]
    me = lax.axis_index("tm")
    for m, piece_ref in enumerate(piece_refs):
        times = piece_ref.shape[0]
        rows = pl.ds(pl.multiple_of((me ^ m) * times, times), times)
        x_ref[rows, :] = piece_ref[...]
    transform_columns(tables, x_ref, *folded, out_ref)


def transform(pieces, tables, slots):
    chunks, times, width = pieces[0].shape
    total = times * len(pieces)
    return pl.pallas_call(
        transform_kernel,
        grid=(chunks,),
        in_specs=[pl.BlockSpec(table.shape, lambda n: (0, 0)) for table in tables]
        + [pl.BlockSpec((None, times, width), lambda n: (n, 0, 0))] * len(pieces),
        out_specs=pl.BlockSpec((None, slots * CHUNK, LANES), lambda n: (n, 0, 0)),
        out_shape=pltpu.HBM((chunks, slots * CHUNK, LANES), F32),
        scratch_shapes=transform_scratch(total, width),
        compiler_params=params(40),
        name="transform",
    )(*tables, *in_hbm(pieces))


def first_lane(chunk, chunks):
    return sum(16 * i + 8 for i in range(chunk + 1, chunks))


GROUP = 8


def chunk_tiles(chunk, chunks, weight, parts, before):
    flipped = jnp.where(low_half(weight.shape), weight, -weight)
    width = CHUNK * (chunk + 1)
    stride = width if LANES % width == 0 else 32
    left, right = [], []
    for row in parts:
        row = row[: chunk + 1]
        right.extend((row + row[-1:])[: stride // CHUNK])
        left.append(row[-1] * weight)
        left.append(pltpu.roll(row[-1], HALF, 1) * flipped)
    lh, ll = split(jnp.concatenate(left, axis=0))
    rh, rl = split(jnp.concatenate(right, axis=0))
    full = lax.dot_general(
        jnp.concatenate([lh, ll, lh], axis=1),
        jnp.concatenate([rh, rh, rl], axis=1),
        (((1,), (1,)), ((), ())),
        preferred_element_type=F32,
    )
    if full.shape[1] < LANES:
        full = jnp.concatenate([full] * (LANES // full.shape[1]), axis=1)
    start = first_lane(chunk, chunks)
    row = lax.broadcasted_iota(jnp.int32, (CHUNK, LANES), 0)
    own = lax.broadcasted_iota(jnp.int32, (CHUNK, LANES), 1) - start
    past = own >= width
    corner = (own >= width - CHUNK) & (own < width) & (own - (width - CHUNK) > row)
    valid = (own >= 0) & (own < width + CHUNK * chunk)
    tiles = []
    for k in range(GROUP):
        first = k * stride // LANES * LANES
        real = full[16 * k : 16 * k + 8, first : first + LANES]
        imag = full[16 * k + 8 : 16 * k + 16, first : first + LANES]
        shift = (start - (k * stride - first)) % LANES
        out = pltpu.roll(real, shift, 1)
        out = jnp.where(corner, pltpu.roll(imag, shift, 1), out)
        out = jnp.where(past, pltpu.roll(imag, (shift + width) % LANES, 1), out)
        tiles.append(jnp.where(valid, out, before[k]))
    return tiles


def early_gram_kernel(tile, chunks, scale, z_ref, w_ref, out_ref):
    weight = w_ref[...] * scale

    def step(g, carry):
        parts = []
        for k in range(GROUP):
            rows = pl.ds(pl.multiple_of((g * GROUP + k) * CHUNK, CHUNK), CHUNK)
            parts.append([z_ref[n, rows, :] for n in range(chunks - 1)])
        tiles = [jnp.zeros((CHUNK, LANES), F32)] * GROUP
        for chunk in range(chunks - 1):
            tiles = chunk_tiles(chunk, chunks, weight, parts, tiles)
        for k in range(GROUP):
            out_ref[g * GROUP + k] = tiles[k]
        return carry

    lax.fori_loop(0, tile // GROUP, step, 0, unroll=True)


def early_gram(spectra, weights, slots, tile, total_points):
    chunks = spectra.shape[0] + 1
    return pl.pallas_call(
        functools.partial(early_gram_kernel, tile, chunks, 1.0 / total_points),
        grid=(slots // tile,),
        in_specs=[
            pl.BlockSpec((chunks - 1, tile * CHUNK, LANES), lambda i: (0, i, 0)),
            pl.BlockSpec((1, LANES), lambda i: (0, 0)),
        ],
        out_specs=pl.BlockSpec((tile, 8, LANES), lambda i: (i, 0, 0)),
        out_shape=pltpu.HBM((slots, 8, LANES), F32),
        compiler_params=params(24),
        name="early_gram",
    )(*in_hbm([spectra]), weights)


def copy_tile(source, buffer, sem, base, size, t):
    there = pl.ds(pl.multiple_of(base + t * size, 8), size)
    here = pl.ds(pl.multiple_of(t * size, 8), size)
    if len(source.shape) == 3 and size % CHUNK == 0 and source.shape[1] != CHUNK:
        return pltpu.make_async_copy(source.at[:, there], buffer.at[:, here], sem)
    return pltpu.make_async_copy(source.at[there], buffer.at[here], sem)


def half_base(half, count):
    return pl.multiple_of((lax.axis_index("space") % 2 ^ half) * count, GROUP)


def late_tiles(tile, weight, early_ref, late_at, before_ref, out_ref, wait):
    chunks = early_ref.shape[0] + 1

    def step(g, carry):
        parts, before = [], []
        for k in range(GROUP):
            start = pl.multiple_of((g * GROUP + k) * CHUNK, CHUNK)
            parts.append([early_ref[n, pl.ds(start, CHUNK), :] for n in range(chunks - 1)])
            parts[-1].append(late_at(start))
            before.append(before_ref[g * GROUP + k])
        tiles = chunk_tiles(chunks - 1, chunks, weight, parts, before)
        for k in range(GROUP):
            out_ref[g * GROUP + k] = tiles[k]
        return carry

    groups = tile // GROUP

    def one_tile(t, carry):
        wait(t)
        return lax.fori_loop(0, groups, lambda g, c: step(t * groups + g, c), carry, unroll=True)

    lax.fori_loop(0, out_ref.shape[0] // tile, one_tile, 0)


def late_first_kernel(tile, scale, *refs):
    tables, w_ref, early, before = refs[:6], refs[6], refs[7], refs[8]
    late_ref, out_ref = refs[-12:-10]
    piece_refs = refs[9:-12]
    x_ref, odd_ref, two_ref, four_ref, z_ref, early_ref, before_ref = refs[-10:-3]
    piece_sems, tile_sems, late_sem = refs[-3:]
    count = out_ref.shape[0]
    base = half_base(1, count)
    me = lax.axis_index("tm")
    arrivals = []
    for m, piece_ref in enumerate(piece_refs):
        times = piece_ref.shape[1]
        rows = pl.ds(pl.multiple_of((me ^ m) * times, times), times)
        arrivals.append(pltpu.make_async_copy(piece_ref.at[0], x_ref.at[rows], piece_sems.at[m]))
        arrivals[-1].start()

    def copies(t):
        first = copy_tile(early, early_ref, tile_sems.at[0, t], base * CHUNK, tile * CHUNK, t)
        return first, copy_tile(before, before_ref, tile_sems.at[1, t], base, tile, t)

    for t in range(count // tile):
        for copy in copies(t):
            copy.start()
    for copy in arrivals:
        copy.wait()
    transform_columns(tables, x_ref, odd_ref, two_ref, four_ref, z_ref)
    keep = pltpu.make_async_copy(z_ref, late_ref.at[0], late_sem)
    keep.start()

    def wait(t):
        for copy in copies(t):
            copy.wait()

    late_at = lambda start: z_ref[pl.ds(pl.multiple_of(base * CHUNK + start, 8), CHUNK), :]
    late_tiles(tile, w_ref[...] * scale, early_ref, late_at, before_ref, out_ref, wait)
    keep.wait()


def late_first(pieces, tables, early, weights, before, slots, tile, total_points):
    _, times, width = pieces[0].shape
    total, count = times * len(pieces), slots // 2
    return pl.pallas_call(
        functools.partial(late_first_kernel, tile, 1.0 / total_points),
        in_specs=[pl.BlockSpec(memory_space=pltpu.VMEM)] * (len(tables) + 1)
        + [pl.BlockSpec(memory_space=pl.ANY)] * (2 + len(pieces)),
        out_specs=[
            pl.BlockSpec(memory_space=pl.ANY),
            pl.BlockSpec(memory_space=pltpu.VMEM),
        ],
        out_shape=[
            pltpu.HBM((1, slots * CHUNK, LANES), F32),
            pltpu.HBM((count, CHUNK, LANES), F32),
        ],
        scratch_shapes=transform_scratch(total, width)
        + [
            pltpu.VMEM((slots * CHUNK, LANES), F32),
            pltpu.VMEM((early.shape[0], count * CHUNK, LANES), F32),
            pltpu.VMEM((count, CHUNK, LANES), F32),
            pltpu.SemaphoreType.DMA((len(pieces),)),
            pltpu.SemaphoreType.DMA((2, count // tile)),
            pltpu.SemaphoreType.DMA(()),
        ],
        compiler_params=params(40),
        name="late_first",
    )(*tables, weights, *in_hbm([early, before, *pieces]))


def late_second_kernel(tile, scale, *refs):
    sources, w_ref, out_ref = refs[:3], refs[3], refs[4]
    buffers, sems = refs[5:8], refs[8]
    count = out_ref.shape[0]
    base = half_base(0, count)
    sizes = (tile * CHUNK, tile * CHUNK, tile)

    def copies(t):
        bases = (base * CHUNK, base * CHUNK, base)
        return [
            copy_tile(sources[n], buffers[n], sems.at[n, t], bases[n], sizes[n], t)
            for n in range(3)
        ]

    for t in range(count // tile):
        for copy in copies(t):
            copy.start()

    def wait(t):
        for copy in copies(t):
            copy.wait()

    late_at = lambda start: buffers[1][0, pl.ds(start, CHUNK), :]
    late_tiles(tile, w_ref[...] * scale, buffers[0], late_at, buffers[2], out_ref, wait)


def late_second(early, late, weights, before, slots, tile, total_points):
    count = slots // 2
    sizes = [(z.shape[0], count * CHUNK, LANES) for z in (early, late)]
    sizes.append((count, CHUNK, LANES))
    return pl.pallas_call(
        functools.partial(late_second_kernel, tile, 1.0 / total_points),
        in_specs=[pl.BlockSpec(memory_space=pl.ANY)] * 3
        + [pl.BlockSpec(memory_space=pltpu.VMEM)],
        out_shape=pltpu.HBM((count, CHUNK, LANES), F32),
        scratch_shapes=[pltpu.VMEM(size, F32) for size in sizes]
        + [pltpu.SemaphoreType.DMA((3, count // tile))],
        compiler_params=params(24),
        name="late_second",
    )(*in_hbm([early, late, before]), weights)


def power_kernel(blocks, x_ref, out_ref):
    count = x_ref.shape[2]
    chunks = blocks // CHUNK
    real = [[None] * chunks for _ in range(chunks)]
    imag = [[None] * chunks for _ in range(chunks)]
    for c in range(chunks):
        start = first_lane(c, chunks)
        for d in range(c):
            x = x_ref[start + CHUNK * d : start + CHUNK * (d + 1)]
            y = x_ref[start + CHUNK * (c + 1 + d) : start + CHUNK * (c + 2 + d)]
            real[d][c], real[c][d] = x, jnp.swapaxes(x, 0, 1)
            imag[d][c], imag[c][d] = y, -jnp.swapaxes(y, 0, 1)
        x = x_ref[start + CHUNK * c : start + CHUNK * (c + 1)]
        flip = jnp.swapaxes(x, 0, 1)
        b = lax.broadcasted_iota(jnp.int32, x.shape, 0)
        s = lax.broadcasted_iota(jnp.int32, x.shape, 1)
        real[c][c] = jnp.where(b <= s, x, flip)
        imag[c][c] = jnp.where(b > s, x, jnp.where(b < s, -flip, 0.0))
    whole = lambda m: jnp.concatenate([jnp.concatenate(r, axis=1) for r in m], axis=0)
    real, imag = whole(real), -whole(imag)

    def apply(vr, vi):
        vr, vi = vr[:, None, :], vi[:, None, :]
        return jnp.sum(real * vr - imag * vi, axis=0), jnp.sum(real * vi + imag * vr, axis=0)

    vr = jnp.full((blocks, count), 1.0 / math.sqrt(blocks), F32)
    vi = jnp.zeros((blocks, count), F32)
    for _ in range(POWER):
        ur, ui = apply(vr, vi)
        length = lax.rsqrt(jnp.sum(ur * ur + ui * ui, axis=0, keepdims=True) + 1e-06)
        vr, vi = ur * length, ui * length
    ur, ui = apply(vr, vi)
    energy = jnp.sum(vr * ur + vi * ui, axis=0, keepdims=True)
    columns = jnp.concatenate([vr, vi, jnp.broadcast_to(energy, (8, count))], axis=0)
    columns = jnp.pad(columns, ((0, LANES - columns.shape[0]), (0, LANES - count)))
    rows = columns.T
    half = count // 2
    low = low_half((half, LANES))
    lane = lax.broadcasted_iota(jnp.int32, (half, LANES), 1)
    first, second = rows[:half], rows[half : 2 * half]
    last = jnp.broadcast_to(rows[2 * half : count], (half, LANES))
    ends = jnp.where(lane == 2, pltpu.roll(last, HALF + 2, 1), pltpu.roll(last, HALF, 1))
    ends = jnp.where(lane == 1, pltpu.roll(second, HALF + 1, 1), ends)
    out_ref[half:] = jnp.where(lane == 0, pltpu.roll(first, HALF, 1), ends)
    out_ref[:half] = jnp.where(low, first, pltpu.roll(second, HALF, 1))


def power(packed, blocks):
    return pl.pallas_call(
        functools.partial(power_kernel, blocks),
        out_shape=jax.ShapeDtypeStruct((packed.shape[2] // 2 * 2, LANES), F32),
        compiler_params=params(32),
        name="power",
    )(packed)


def reverse_rows(value):
    row = lax.broadcasted_iota(jnp.int32, (8, LANES), 0)
    tiles = []
    for start in range(0, value.shape[0], 8):
        tile = value[start : start + 8]
        for span in (1, 2, 4):
            upper = (row & span) == 0
            tile = jnp.where(upper, pltpu.roll(tile, 8 - span, 0), pltpu.roll(tile, span, 0))
        tiles.append(tile)
    return jnp.concatenate(tiles[::-1], axis=0)


def unpack_vectors(packed_ref, v_ref, classes):
    devices, rows, _ = packed_ref.shape
    half = rows // 2
    count = v_ref.shape[0] // devices
    spaces = devices // classes
    low = low_half((half, LANES))
    for device in range(devices):
        tau, space = divmod(device, spaces)
        order = bit_reverse(space, spaces.bit_length() - 1)
        start = (order * classes + tau) * count
        vector, ends = packed_ref[device, :half, :], packed_ref[device, half:, :]
        turned = pltpu.roll(ends, HALF, 1)
        v_ref[start : start + half, :] = jnp.where(low, vector, turned)
        second = jnp.where(low, pltpu.roll(vector, HALF, 1), pltpu.roll(ends, HALF - 1, 1))
        v_ref[start + half : start + 2 * half, :] = second
        last = jnp.where(low, turned, pltpu.roll(ends, HALF - 2, 1))
        v_ref[start + 2 * half : start + count, :] = last[:1]


def modes_kernel(tile, classes, total_times, *refs):
    early, late, packed_ref, out_ref, energy_ref, z_ref, s_ref, e_ref, v_ref, sems = refs
    chunks = z_ref.shape[0]
    blocks = CHUNK * z_ref.shape[0]
    group = 8
    lane = lax.broadcasted_iota(jnp.int32, (group, LANES), 1)
    row = lax.broadcasted_iota(jnp.int32, (group, LANES), 0)
    per_tile = LANES // blocks
    low = low_half((group, LANES))

    def spread(vector):
        vector = jnp.where(lane < blocks, vector, 0.0)
        span = blocks
        while span < LANES:
            vector = vector + pltpu.roll(vector, span, 1)
            span *= 2
        parts = []
        for first in range(0, group, per_tile):
            parts.append(jnp.where(lane // blocks + first == row, vector, 0.0))
        return jnp.concatenate(parts, axis=1)

    def step(g, carry):
        start = pl.multiple_of(g * group, group)
        vec = v_ref[pl.ds(start, group), :]
        both = jnp.concatenate([spread(vec), spread(pltpu.roll(vec, LANES - blocks, 1))], axis=0)
        vh, vl = split(both)
        z = []
        for k in range(group):
            rows = pl.ds(pl.multiple_of((g * group + k) * CHUNK, CHUNK), CHUNK)
            z.append(z_ref[:, rows, :].reshape(blocks, LANES))
        zh, zl = split(jnp.concatenate(z, axis=0))
        full = jnp.dot(
            jnp.concatenate([vh, vl], axis=0),
            jnp.concatenate([zh, zl], axis=1),
            preferred_element_type=F32,
        )
        sums = full[:16, :LANES] + full[:16, LANES:] + full[16:, :LANES]
        turned = pltpu.roll(sums[8:], HALF, 1)
        value = sums[:8] + jnp.where(low, -turned, turned)
        energy = jnp.broadcast_to(vec[:, 2 * blocks : 2 * blocks + 1], (group, LANES))
        s_ref[pl.ds(start, group), :] = value * lax.rsqrt(energy + 1e-06)
        e_ref[pl.ds(start, group), :] = energy
        return carry

    groups = tile // group
    tiles = v_ref.shape[0] // tile

    def copies(t):
        rows = pl.ds(pl.multiple_of(t * tile * CHUNK, CHUNK), tile * CHUNK)
        first, second = z_ref.at[: chunks - 1, rows], z_ref.at[chunks - 1 :, rows]
        return (
            pltpu.make_async_copy(early.at[:, rows], first, sems.at[0, t]),
            pltpu.make_async_copy(late.at[:, rows], second, sems.at[1, t]),
        )

    for t in range(tiles):
        for copy in copies(t):
            copy.start()
    unpack_vectors(packed_ref, v_ref, classes)

    def one_tile(t, carry):
        for copy in copies(t):
            copy.wait()
        return lax.fori_loop(0, groups, lambda g, c: step(t * groups + g, c), carry, unroll=True)

    lax.fori_loop(0, tiles, one_tile, 0)

    half = out_ref.shape[0] // classes // 2
    bits = classes.bit_length() - 1
    low = low_half((half, LANES))
    for d in range(classes):
        r = bit_reverse(d, bits)
        direct = pl.ds(slot_of(r, total_times), half, stride=classes // 4)
        mirror = pl.ds(slot_of(classes - r, total_times), half, stride=classes // 4)
        start = 2 * half * d
        out_ref[start : start + half, :] = s_ref[direct, :]
        energy_ref[start : start + half, :] = e_ref[direct, :]
        turned = reverse_rows(s_ref[mirror, :])
        out_ref[start + half : start + 2 * half, :] = jnp.where(low, turned, -turned)
        energy_ref[start + half : start + 2 * half, :] = reverse_rows(e_ref[mirror, :])


def modes(early, late, vectors, total, classes, slots, tile):
    return pl.pallas_call(
        functools.partial(modes_kernel, tile, classes, total),
        in_specs=[
            pl.BlockSpec(memory_space=pl.ANY),
            pl.BlockSpec(memory_space=pl.ANY),
            pl.BlockSpec(memory_space=pltpu.VMEM),
        ],
        out_shape=[jax.ShapeDtypeStruct((total, LANES), F32)] * 2,
        scratch_shapes=[
            pltpu.VMEM((early.shape[0] + 1, *early.shape[1:]), F32),
            pltpu.VMEM((slots, LANES), F32),
            pltpu.VMEM((slots, LANES), F32),
            pltpu.VMEM((slots, LANES), F32),
            pltpu.SemaphoreType.DMA((2, slots // tile)),
        ],
        compiler_params=params(24),
        name="modes",
    )(*in_hbm([early, late]), vectors)


def place_kernel(x_ref, out_ref):
    low = low_half(x_ref.shape[1:])
    for i in range(x_ref.shape[0] // 2):
        first, second = x_ref[2 * i], x_ref[2 * i + 1]
        cols = slice(i * LANES, (i + 1) * LANES)
        out_ref[0, :, cols] = jnp.where(low, first, pltpu.roll(second, HALF, 1))
        out_ref[1, :, cols] = jnp.where(low, pltpu.roll(first, HALF, 1), second)


def place(pieces):
    count, rows, _ = pieces.shape
    return pl.pallas_call(
        place_kernel,
        out_shape=jax.ShapeDtypeStruct((2, rows, count * HALF), F32),
        compiler_params=params(32),
        name="place",
    )(pieces)


def exchange(value, axes):
    return lax.all_to_all(value, axes, 0, 0, tiled=True)


def body(mesh_shape, snapshots, quad_weights):
    tm_size, space_size = mesh_shape["tm"], mesh_shape["space"]
    local_times, blocks, points = snapshots.shape
    total_times = local_times * tm_size
    total_points = points * space_size
    devices = tm_size * space_size
    per_device = -(-(total_times // 2 + 1) // devices)
    slots = per_device * devices
    tile = slots // 4
    tables = transform_tables(total_times, slots)
    window = jnp.asarray(window_table(total_times))

    here = lax.axis_index("tm") * HALF
    weights = lax.dynamic_slice(quad_weights, (here,), (HALF,))
    weights = jnp.concatenate([weights, weights])[None, :]

    chunks = blocks // CHUNK

    def send(group, offsets, after):
        sent = dict(zip(offsets, pack(snapshots, window, group, tuple(offsets), after)))
        flying = {}
        for m, part in sent.items():
            pairs = [(d, d ^ m) for d in range(tm_size)]
            flying[m] = lax.ppermute(part, "tm", pairs) if m else part
        return sent, flying

    half, quarter = tm_size // 2, tm_size // 4
    first = [*range(half, half + quarter), *range(quarter)]
    second = [*range(half + quarter, tm_size), *range(quarter, half)]
    group = range(chunks - 1)
    sent, pieces = send(group, first[:1], [])
    sent, more = send(group, first[1:], [sent[half]])
    pieces |= more
    pieces |= send(group, second, [sent[0]])[1]
    group = range(chunks - 1, chunks)
    sent, last = send(group, first, [pieces[half]])
    last |= send(group, second, [sent[0], pieces[half + quarter]])[1]
    ordered = lambda pieces: [pieces[m] for m in range(tm_size)]
    early = transform(ordered(pieces), tables, slots)
    matrices = early_gram(early, weights, slots, tile, total_points)
    late, given = late_first(
        ordered(last), tables, early, weights, matrices, slots, tile, total_points
    )

    space = lax.axis_index("space")

    def swap(value, level):
        pairs = [(i, i ^ (1 << level)) for i in range(space_size)]
        return lax.ppermute(value, "space", pairs)

    arriving = swap(given, 0)
    part = late_second(early, late, weights, matrices, slots, tile, total_points)
    levels = space_size.bit_length() - 1
    shape = (*[2] * (levels - 1), tm_size, per_device, *part.shape[1:])
    part, arriving = part.reshape(shape), arriving.reshape(shape)
    bit = space // 2
    pick = lambda value, i: lax.dynamic_index_in_dim(value, i, 0, keepdims=False)
    cut = 3 * per_device // 4 + 2
    given = pick(part, 1 - bit)[:, :cut] + pick(arriving, 1 - bit)[:, :cut]
    kept = pick(part, bit)[:, :cut] + pick(arriving, bit)[:, :cut]
    given = swap(given, 1)
    rest = part[:, :, cut:] + arriving[:, :, cut:]
    rest = lax.all_to_all(rest, "tm", 1, 1, tiled=True).sum(axis=1)
    rest = pick(rest, bit) + swap(pick(rest, 1 - bit), 1)
    part = exchange(kept + given, "tm").sum(axis=0)
    part = jnp.concatenate([part, rest], axis=0)

    vectors = power(part.transpose(2, 1, 0), blocks)
    vectors = jnp.broadcast_to(vectors[None], (devices, *vectors.shape))
    vectors = exchange(vectors, ("tm", "space"))

    pieces, energies = modes(early, late, vectors, total_times, tm_size, slots, tile)
    pieces = exchange(pieces.reshape(tm_size, local_times, LANES), "tm")
    energies = energies.reshape(tm_size, local_times, LANES)[:, :, 0]
    energies = lax.dynamic_index_in_dim(energies, lax.axis_index("tm"), 0, keepdims=False)
    return place(pieces), energies


def fits(mesh_shape, times, blocks, points):
    tm_size, space_size = mesh_shape["tm"], mesh_shape["space"]
    return (
        points == space_size * tm_size * HALF
        and (tm_size, space_size) == (8, 4)
        and times % (tm_size * 8) == 0
        and blocks % CHUNK == 0
        and blocks == 32
    )


def matvec(matrix, vector):
    return jnp.einsum("fbc,fc->fb", matrix, vector, precision=lax.Precision.HIGHEST)


def power_modes(real_gram, imag_gram):
    vec_real = jnp.ones(real_gram.shape[:2], jnp.float32) / math.sqrt(real_gram.shape[1])
    vec_imag = jnp.zeros(real_gram.shape[:2], jnp.float32)
    for sweep_idx in range(POWER):
        new_real = matvec(real_gram, vec_real) - matvec(imag_gram, vec_imag)
        new_imag = matvec(real_gram, vec_imag) + matvec(imag_gram, vec_real)
        length = lax.rsqrt(
            jnp.sum(new_real * new_real + new_imag * new_imag, axis=1, keepdims=True) + 1e-06
        )
        vec_real = new_real * length
        vec_imag = new_imag * length
    image_real = matvec(real_gram, vec_real) - matvec(imag_gram, vec_imag)
    image_imag = matvec(real_gram, vec_imag) + matvec(imag_gram, vec_real)
    energy = jnp.sum(vec_real * image_real + vec_imag * image_imag, axis=1)
    return (vec_real, vec_imag, energy)


def general_body(snapshots, quad_weights):
    tm_size = lax.axis_size("tm")
    bit_count = tm_size.bit_length() - 1
    local_times, blocks, points = snapshots.shape
    total_times = local_times * tm_size
    total_points = points * lax.axis_size("space")
    norm_factor = 1.0 / math.sqrt(0.375 * total_times)
    flattened = snapshots.reshape(local_times, blocks * points)
    columns = lax.all_to_all(flattened, "tm", split_axis=1, concat_axis=0, tiled=True)
    col_count = columns.shape[1]
    times_all = jnp.arange(total_times, dtype=jnp.int32)
    window = (
        0.5 - 0.5 * jnp.cos(2.0 * math.pi * times_all.astype(jnp.float32) / total_times)
    ) * norm_factor
    row_block = min(256, total_times)

    def one_block(block_idx):
        row_ids = block_idx * row_block + jnp.arange(row_block, dtype=jnp.int32)
        frequency = bit_reverse(row_ids // local_times, bit_count) + tm_size * (
            row_ids % local_times
        )
        angles = (
            -2.0
            * math.pi
            * (frequency[:, None] * times_all[None, :] % total_times).astype(jnp.float32)
            / total_times
        )
        cos_tab = jnp.cos(angles) * window[None, :]
        sin_tab = jnp.sin(angles) * window[None, :]
        return (
            jnp.dot(cos_tab, columns, precision=lax.Precision.HIGHEST),
            jnp.dot(sin_tab, columns, precision=lax.Precision.HIGHEST),
        )

    spec_real, spec_imag = lax.map(one_block, jnp.arange(total_times // row_block, dtype=jnp.int32))
    spectrum = jnp.stack(
        [spec_real.reshape(total_times, col_count), spec_imag.reshape(total_times, col_count)]
    )
    returned = lax.all_to_all(spectrum, "tm", split_axis=1, concat_axis=2, tiled=True)
    spectral = returned.reshape(2, local_times, blocks, points)
    weighted = spectral * quad_weights
    gram_full = (
        jnp.einsum("pfbx,qfcx->fpbqc", weighted, spectral, precision=lax.Precision.HIGHEST)
        / total_points
    )
    real_gram = gram_full[:, 0, :, 0] + gram_full[:, 1, :, 1]
    imag_gram = gram_full[:, 0, :, 1] - gram_full[:, 1, :, 0]
    real_gram, imag_gram = lax.psum((real_gram, imag_gram), "space")
    vec_real, vec_imag, energy = power_modes(real_gram, imag_gram)
    inverse_root = lax.rsqrt(energy + 1e-06)[:, None]
    modes_real = jnp.einsum(
        "fb,fbx->fx", vec_real, spectral[0], precision=lax.Precision.HIGHEST
    ) - jnp.einsum("fb,fbx->fx", vec_imag, spectral[1], precision=lax.Precision.HIGHEST)
    modes_imag = jnp.einsum(
        "fb,fbx->fx", vec_imag, spectral[0], precision=lax.Precision.HIGHEST
    ) + jnp.einsum("fb,fbx->fx", vec_real, spectral[1], precision=lax.Precision.HIGHEST)
    return (jnp.stack([modes_real * inverse_root, modes_imag * inverse_root]), energy)


def solution(mesh):
    shape = dict(mesh.shape)

    def program(snapshots, quad_weights):
        chosen = general_body
        if fits(shape, *snapshots.shape):
            chosen = functools.partial(body, shape)
        return jax.shard_map(
            chosen,
            mesh=mesh,
            in_specs=(P("tm", None, "space"), P("space")),
            out_specs=(P(None, "tm", "space"), P("tm")),
            check_vma=False,
        )(snapshots, quad_weights)

    return program
```
